512 devices in a mesh: bt: 64 (over z, x), ch: 8 (over y, core).
Axes of the slice: x: 4, y: 4, z: 16, core: 2. Of those that a mesh axis runs over, the one named last changes fastest.
Arguments:
- visibility: float32 [2, 4, 64, 16384], P(None, None, 'ch', 'bt'), may hold values from -6 to 6
- cell_offset: float32 [2, 4, 64, 16384], P(None, None, 'ch', 'bt'), may hold values from 2 to 30
- station_gain: float32 [2, 64, 512], P(None, 'ch'), may hold values from 0.1 to 1.9
- stations: int32 [16384, 2], P('bt'), may hold values from 0 to 511, all different within a row
- row_band: int32 [16384, 1], replicated, may hold values from 0 to 63; in each aligned block of 32 rows (0 to 31, 32 to 63, ...) at most 2 rows name the same one
- tile_offset: int32 [16384], replicated, may hold values from 0 to 127
Outputs:
- sky_image: float32 [2, 8192, 8192], P(None, ('bt', 'ch'))
The draws below stay inside these ranges and needn't reach their ends.
Inputs may be any that keep to these rules, and one draw needn't show every extreme that they name: `row_band`: in each aligned run of 32 blocks (one bt index's blocks of one column band) no row band is named by more than 2 blocks. The two stations of a block differ.
All inputs are finite; a program needn't handle non-finite values.
Results may differ from the reference program's by a relative error of at most 0.0003.
Values sent between devices are 32-bit elements; how exact they have to be, the bound alone decides.
A program may use at most 64 MiB of HBM per device.

```python
import math
import jax
import jax.numpy as jnp
import numpy as np
from jax import lax

SUB = 32
TSLOT = 4
CHANNELS = 64
STATIONS = 512
NB = 256
BLOCKS = 16384
NBC = 32
G = 8192
GT = 256
TRB = 4
TCB = 32
CAPR = 2
N_BT = 64


def place_ends(entries, rng, smallest, high):
    index_at = [jax.random.randint(jax.random.fold_in(rng, axis), (), 0, length) for axis, length in enumerate(entries.shape)]
    widest = entries.shape.index(max(entries.shape))
    neighbour = index_at[:widest] + [(index_at[widest] + 1) % entries.shape[widest]] + index_at[widest + 1:]
    return entries.at[tuple(index_at)].set(smallest).at[tuple(neighbour)].set(high)


def levels(rng, extent, cuts, least, largest):
    def one(axis_at, blocks):
        draws = jax.random.uniform(jax.random.fold_in(jax.random.fold_in(rng, 6), axis_at), (blocks,), jnp.float32, least / len(cuts), largest / len(cuts))
        return jnp.repeat(jnp.exp(draws), extent[axis_at] // blocks).reshape((-1,) + (1,) * (len(extent) - axis_at - 1))

    factor_of = one(*cuts[0])
    for cut in cuts[1:]:
        factor_of = factor_of * one(*cut)
    return factor_of


def different_ones(rng, rows, amount, top, lift):
    ranking = jax.random.permutation(jax.random.fold_in(rng, 1), amount)
    favour = ranking
    for power in range(3):
        favour = favour * favour // amount
    favour = favour * lift // amount
    chance = jax.random.randint(jax.random.fold_in(rng, 2), (rows, amount), 0, 4096) + favour
    holders = jax.random.permutation(jax.random.fold_in(rng, 3), rows)[jnp.arange(amount) % rows]
    chance = jnp.where(jnp.arange(rows)[:, None] == holders[None, :], 1 << 14, chance)
    merit = chance * amount + jnp.arange(amount)
    return lax.top_k(merit.astype(jnp.int32), top)[1].astype(jnp.int32)


def shared_out(own_key, own, number, rows, amount, top, reach, slope):
    ranking = jax.random.permutation(own_key, amount)
    heavy_load, common = shares(amount, rows * top, reach, slope, True), shares(amount, rows * top, reach, slope, False)
    places = jnp.arange(amount)

    def named(lengths, turn):
        used = int((lengths > 0).sum())
        fixed = max(1, used // 4)
        moved = fixed + (places - fixed + turn * (used - fixed)) % max(1, amount - fixed)
        return jnp.zeros((amount,), jnp.int32).at[ranking[jnp.where(places < fixed, places, moved)]].set(jnp.asarray(lengths, jnp.int32))

    lengths = jnp.where(number % 4 == 0, named(heavy_load, number // 4), named(common, number - number // 4 - 1))
    mixed = jax.random.permutation(jax.random.fold_in(own, 3), amount)
    giver, taker = mixed[0:amount // 2 * 2:2], mixed[1:amount // 2 * 2:2]
    slack = jnp.minimum(lengths[giver] - 1, reach - lengths[taker]) // 2
    slack = jnp.where((giver == ranking[0]) | (taker == ranking[0]) | (lengths[taker] == 0), 0, jnp.maximum(slack, 0))
    moved = jax.random.randint(jax.random.fold_in(own, 4), (amount // 2,), 0, 1 << 20) % (slack + 1)
    lengths = lengths.at[giver].add(-moved).at[taker].add(moved)
    members = jnp.searchsorted(jnp.cumsum(lengths), jnp.arange(rows * top), side="right").astype(jnp.int32)
    table = members.reshape(top, rows).T
    table = table[jax.random.permutation(jax.random.fold_in(own, 1), rows)]
    turn = jax.random.randint(jax.random.fold_in(own, 2), (rows, 1), 0, top)
    return jnp.take_along_axis(table, (jnp.arange(top)[None, :] + turn) % top, axis=1)


def shares(number_of, total, reach, lean, full):
    portions = [(1 << 20) // math.isqrt(standing ** lean) + 1 for standing in range(1, number_of + 1)]
    largest = reach if full else min(reach, max(-(-total // number_of), total * portions[0] // sum(portions)))
    least = 1 if total - largest >= number_of - 1 else 0
    counts, spare = [largest] + [least] * (number_of - 1), total - largest - least * (number_of - 1)
    while spare > 0:
        movable = [i for i in range(1, number_of) if counts[i] < largest] or [i for i in range(1, number_of) if counts[i] < reach]
        mass, left = sum([portions[i] for i in movable]), spare
        for i in movable:
            extra = min(reach - counts[i], max(1, left * portions[i] // mass), spare)
            counts[i] = counts[i] + extra
            spare = spare - extra
    return np.array(counts)


def normal_values(stream_key, shape, width, reach, shards=(), held_as=jnp.bfloat16):
    factor_of = levels(stream_key, shape, shards, -0.22, 0.18) if shards else 1.0
    drawn = jax.random.normal(stream_key, shape, jnp.float32) * width * factor_of
    return jnp.minimum(jnp.maximum(drawn, -reach), reach).astype(held_as)


def setup_inputs(seed: int = 0) -> dict:
    arg_keys = jax.random.split(jax.random.key(seed), 7)
    visibility = normal_values(arg_keys[0], (2, TSLOT, CHANNELS, BLOCKS), 1.0, 6.0, ((2, 8), (3, 64)), jnp.float32)
    cell_offset = jnp.clip(2.0 + 28.0 * jax.random.uniform(arg_keys[1], (2, TSLOT, CHANNELS, BLOCKS), jnp.float32) ** levels(arg_keys[1], (2, TSLOT, CHANNELS, BLOCKS), ((2, 8), (3, 64)), -0.2, 0.2), 2.0, 30.0)
    station_gain = jnp.clip(1.0 + 0.18 * jax.random.normal(arg_keys[2], (2, CHANNELS, STATIONS), jnp.float32), 0.1, 1.9)
    stations = different_ones(arg_keys[3], BLOCKS, STATIONS, 2, 0)
    row_band_keys = jax.random.split(jax.random.fold_in(arg_keys[4], 1), BLOCKS // NBC)
    row_band_turns = jax.random.permutation(jax.random.fold_in(arg_keys[4], 3), BLOCKS // NBC)
    row_band = jax.vmap(lambda own, number: shared_out(jax.random.fold_in(arg_keys[4], 2), own, number, NBC, N_BT, 1, CAPR, 2))(row_band_keys, row_band_turns).reshape((BLOCKS, 1))
    tile_offset = place_ends(jax.random.randint(arg_keys[5], (BLOCKS,), 0, TRB * TCB), jax.random.fold_in(arg_keys[5], 1), 0, (TRB * TCB) - 1).astype(jnp.int32)
    return {"visibility": visibility, "cell_offset": cell_offset, "station_gain": station_gain, "stations": stations, "row_band": row_band, "tile_offset": tile_offset}


highest = lax.Precision.HIGHEST
full_turn = 2.0 * math.pi

def complex_einsum(form, left_side, right_side):
    real_part = jnp.einsum(form, left_side[0], right_side[0], precision=highest) - jnp.einsum(form, left_side[1], right_side[1], precision=highest)
    imag_part = jnp.einsum(form, left_side[0], right_side[1], precision=highest) + jnp.einsum(form, left_side[1], right_side[0], precision=highest)
    return jnp.stack([real_part, imag_part])

def centred_offsets(length):
    return (jnp.arange(length, dtype=jnp.float32) - length // 2) / length

def phasor_pair(coords, length):
    angles = (full_turn * centred_offsets(length))[None, :, None] * coords[:, None, :]
    return jnp.stack([jnp.cos(angles), jnp.sin(angles)])

def tile_table(length):
    positions = jnp.arange(length, dtype=jnp.int32)
    product = positions[:, None] * (positions[None, :] - length // 2) % length
    angles = -full_turn * product.astype(jnp.float32) / length
    centred = centred_offsets(length)
    tapers = jnp.exp(-4.0 * centred * centred) / math.sqrt(length)
    return jnp.stack([jnp.cos(angles) * tapers[None, :], jnp.sin(angles) * tapers[None, :]])

def weighted_vis(visibility, gain_first, gain_second):
    product_real = gain_first[0] * gain_second[0] + gain_first[1] * gain_second[1]
    product_imag = gain_first[1] * gain_second[0] - gain_first[0] * gain_second[1]
    real_part = visibility[0] * product_real[None] - visibility[1] * product_imag[None]
    imag_part = visibility[0] * product_imag[None] + visibility[1] * product_real[None]
    return jnp.stack([real_part, imag_part])

def image_subgrids(weighted, coords):
    phase_first = phasor_pair(coords[0], SUB)
    phase_second = phasor_pair(coords[1], SUB)
    scaled = jnp.stack([weighted[0][:, None, :] * phase_first[0] - weighted[1][:, None, :] * phase_first[1], weighted[0][:, None, :] * phase_first[1] + weighted[1][:, None, :] * phase_first[0]])
    return complex_einsum('klb,kmb->lmb', scaled, phase_second)

def to_tiles(subgrid_image):
    factor_table = tile_table(SUB)
    partial_value = complex_einsum('pl,lmb->pmb', factor_table, subgrid_image)
    return complex_einsum('qm,pmb->pqb', factor_table, partial_value)

def reference(visibility, cell_offset, station_gain, stations, row_band, tile_offset):
    gain_first = station_gain[:, :, stations[:, 0]]
    gain_second = station_gain[:, :, stations[:, 1]]
    weighted = weighted_vis(visibility, gain_first, gain_second)
    grouped_weights = weighted.reshape(2, TSLOT * CHANNELS, N_BT, NB).transpose(2, 0, 1, 3)
    grouped_coords = cell_offset.reshape(2, TSLOT * CHANNELS, N_BT, NB).transpose(2, 0, 1, 3)

    def one_group(packed):
        return to_tiles(image_subgrids(packed[0], packed[1]))
    tile_stack = lax.map(one_group, (grouped_weights, grouped_coords))
    tile_stack = tile_stack.transpose(0, 4, 1, 2, 3).reshape(BLOCKS, 2, SUB, SUB)
    block_index = jnp.arange(BLOCKS, dtype=jnp.int32)
    tile_row = row_band[:, 0] * TRB + tile_offset // TCB
    tile_column = block_index % NB // NBC * TCB + tile_offset % TCB
    grid_cells = jnp.zeros((GT, GT, 2, SUB, SUB), jnp.float32).at[tile_row, tile_column].add(tile_stack)
    grid_cells = grid_cells.transpose(2, 0, 3, 1, 4).reshape(2, G, G)
    complex_grid = lax.complex(grid_cells[0], grid_cells[1])
    sky_values = jnp.fft.ifft2(complex_grid) * (G / math.sqrt(TSLOT * CHANNELS))
    return jnp.stack([jnp.real(sky_values), jnp.imag(sky_values)]).astype(jnp.float32)
```

```python
import math

import jax
import jax.numpy as jnp
import ml_dtypes
import numpy as np
from jax import lax
from jax.experimental import pallas as pl
from jax.experimental.pallas import tpu as pltpu
from jax.sharding import PartitionSpec as P

MESH = pl.DeviceIdType.MESH
NZ, NX, NCH = 16, 4, 8
SUB = 32
G = 8192
SPAN = G // NZ
BF = jnp.bfloat16
F32 = jnp.float32


def split_const(table):
    high = np.asarray(table, np.float32).astype(ml_dtypes.bfloat16)
    low = (np.asarray(table, np.float64) - high.astype(np.float64)).astype(np.float32).astype(ml_dtypes.bfloat16)
    return high, low


def taper_dft():
    pos = np.arange(SUB)
    x = (pos - SUB // 2) / SUB
    return np.exp(-2j * np.pi * np.outer(pos, x)) * (np.exp(-4.0 * x * x) / math.sqrt(SUB))[None, :]


def front_table():
    table = taper_dft()
    high, low = split_const(np.concatenate([table.real, table.imag], 0))
    return np.concatenate([high, high, low], 1)


def row_table():
    a = np.arange(G)
    u = np.exp(2j * np.pi * np.outer(a, np.arange(SUB)) / G) @ taper_dft()
    u = u.reshape(NZ, SPAN, SUB).transpose(0, 2, 1)
    w = np.concatenate(
        [np.concatenate([u.real, u.imag], 2), np.concatenate([-u.imag, u.real], 2)], 1
    )
    high, low = split_const(w)
    return np.concatenate([high, high, low, low], 1)


def row_phase():
    ang = 2 * np.pi * (np.outer(np.arange(256), np.arange(256)) % 256) / 256
    return np.concatenate([np.cos(ang), np.sin(ang)], 1).astype(np.float32)


def column_table():
    ang = 2 * np.pi * (np.outer(np.arange(256), np.arange(256)) % 256) / 256
    c, s = np.cos(ang), np.sin(ang)
    return split_const(np.concatenate([np.concatenate([c, s], 1), np.concatenate([-s, c], 1)], 0))


def column_twiddle():
    ang = 2 * np.pi * np.outer(np.arange(SUB), np.arange(256)) / G
    scale = 1.0 / (G * 16.0)
    return (np.concatenate([np.cos(ang), np.sin(ang)], 1) * scale).astype(np.float32)


def trig_coefficients():
    f = 0.5 * np.cos(np.pi * (np.arange(4000) + 0.5) / 4000)
    y = f * f
    cosine = np.polynomial.chebyshev.Chebyshev.fit(y, np.cos(2 * np.pi * f), 8, domain=[0, 0.25])
    sine = np.polynomial.chebyshev.Chebyshev.fit(
        y, np.sin(2 * np.pi * f) / f, 7, domain=[0, 0.25]
    )
    convert = np.polynomial.Polynomial
    return (
        [float(v) for v in cosine.convert(kind=convert).coef],
        [float(v) for v in sine.convert(kind=convert).coef],
    )


COS_C, SIN_C = trig_coefficients()


def horner(coefs, y):
    total = jnp.full_like(y, coefs[-1])
    for value in coefs[-2::-1]:
        total = total * y + value
    return total


def phasor(turns):
    f = turns - jnp.floor(turns + 0.5)
    y = f * f
    return horner(COS_C, y), f * horner(SIN_C, y)


def halves(v):
    high = v.astype(BF)
    return high, (v - high.astype(F32)).astype(BF)


def dot(a, b, dims=((1,), (0,))):
    return lax.dot_general(a, b, (dims, ((), ())), preferred_element_type=F32)


def lanes(shape):
    return lax.broadcasted_iota(jnp.int32, shape, 1)


def front_kernel(
    vis, off, gain, st, ttab, out,
    packed, landed, quant, image, tile,
    ch_send, ch_recv, x_send, x_recv, z_send, z_recv,
):
    bt, ch = lax.axis_index("bt"), lax.axis_index("ch")
    z, x = bt // NX, bt % NX
    ch_peer = [(bt, (ch + d) % NCH) for d in range(1, NCH)]
    x_peer = [(z * NX + (x + d) % NX, ch) for d in range(1, NX)]
    right = (((z + 1) % NZ) * NX + x, ch)
    left = (((z + NZ - 1) % NZ) * NX + x, ch)
    barrier = pltpu.get_barrier_semaphore()
    peers = ch_peer + x_peer + [right, left]
    for peer in peers:
        pl.semaphore_signal(barrier, inc=1, device_id=peer, device_id_type=MESH)

    g = gain[...]
    g0 = g.astype(BF)
    rest = g - g0.astype(F32)
    g1 = rest.astype(BF)
    g2 = (rest - g1.astype(F32)).astype(BF)
    parts = jnp.concatenate([g0, g1, g2], 0)
    stations = lax.broadcasted_iota(jnp.int32, (512, 256), 0)

    def pick(row):
        hot = jnp.where(stations == st[row : row + 1, :], 1.0, 0.0).astype(BF)
        got = dot(parts, hot)
        got = (got[0:16] + got[16:32]) + got[32:48]
        return got[0:8], got[8:16]

    pr, pi = pick(0)
    qr, qi = pick(1)
    ar = pr * qr + pi * qi
    ai = pi * qr - pr * qi
    rows_r, rows_i, rows_u, rows_v = [], [], [], []
    for t in range(4):
        vr, vi = vis[0, t], vis[1, t]
        rows_r.append(vr * ar - vi * ai)
        rows_i.append(vr * ai + vi * ar)
        rows_u.append(off[0, t])
        rows_v.append(off[1, t])
    packed[...] = jnp.concatenate(rows_r + rows_i + rows_u + rows_v, 0).T
    landed[ch] = packed[pl.ds(pl.multiple_of(ch * 32, 32), 32), :]

    pl.semaphore_wait(barrier, len(peers))
    copies = []
    for d, peer in enumerate(ch_peer):
        copy = pltpu.make_async_remote_copy(
            src_ref=packed.at[pl.ds(pl.multiple_of(peer[1] * 32, 32), 32)],
            dst_ref=landed.at[ch],
            send_sem=ch_send.at[d],
            recv_sem=ch_recv.at[d],
            device_id=peer,
            device_id_type=MESH,
        )
        copy.start()
        copies.append(copy)
    for copy in copies:
        copy.wait()

    lane = lanes((32, 128))
    for h in range(2):
        for q in range(4):
            got = None
            for i in range(4):
                shift = (32 * (i - q)) % 128
                piece = landed[4 * h + i]
                if shift:
                    piece = pltpu.roll(piece, shift, 1)
                got = piece if got is None else jnp.where(lane >= 32 * i, piece, got)
            quant[q, :, 128 * h : 128 * h + 128] = got

    xl = (lax.broadcasted_iota(jnp.int32, (32, 256), 0) - 16).astype(F32) * (1.0 / 32.0)
    sign = jnp.where((lane // 32) % 2 == 0, -1.0, 1.0)

    def one_block(b):
        wr = quant[0, pl.ds(b, 1), :]
        wi = quant[1, pl.ds(b, 1), :]
        u = quant[2, pl.ds(b, 1), :]
        v = quant[3, pl.ds(b, 1), :]
        cu, su = phasor(xl * u)
        rr, ri = phasor(xl * v)
        lr = wr * cu - wi * su
        li = wr * su + wi * cu
        lrh, lrl = halves(lr)
        lih, lil = halves(li)
        rrh, rrl = halves(rr)
        rih, ril = halves(ri)
        d = dot(
            jnp.concatenate([rrh, rih, rrl, ril], 0),
            jnp.concatenate([lrh, lih, lrl, lil], 0),
            ((1,), (1,)),
        )
        pr_ = d[0:32] + d[64:96]
        pi_ = d[32:64] + d[96:128]
        pr_ = pr_ + pltpu.roll(pr_, 64, 1)
        pi_ = pi_ + pltpu.roll(pi_, 64, 1)
        return pr_ + sign * pltpu.roll(pi_, 32, 1)

    def pair(p, carry):
        both = jnp.where(lane < 64, one_block(2 * p), one_block(2 * p + 1))
        image[:, pl.ds(pl.multiple_of(p * 128, 128), 128)] = both
        return carry

    lax.fori_loop(0, 16, pair, 0)

    def to_tile(p, carry):
        at = pl.ds(pl.multiple_of(p * 256, 256), 256)
        high, low = halves(image[:, at])
        ts = dot(ttab[...], jnp.concatenate([high, low, high], 0))
        for k in range(2):
            tr = ts[0:32, 128 * k : 128 * k + 128]
            ti = ts[32:64, 128 * k : 128 * k + 128]
            other = jnp.where(sign < 0, pltpu.roll(ti, 96, 1), pltpu.roll(ti, 32, 1))
            tile[:, pl.ds(pl.multiple_of(p * 256 + 128 * k, 128), 128)] = tr + sign * other
        return carry

    lax.fori_loop(0, 8, to_tile, 0)

    copies = []
    for d, peer in enumerate(x_peer):
        to = (x + d + 1) % NX
        copy = pltpu.make_async_remote_copy(
            src_ref=tile.at[pl.ds(pl.multiple_of(to * 8, 8), 8)],
            dst_ref=out.at[z, x],
            send_sem=x_send.at[d],
            recv_sem=x_recv.at[d],
            device_id=peer,
            device_id_type=MESH,
        )
        copy.start()
        copies.append(copy)
    out[z, x] = tile[pl.ds(pl.multiple_of(x * 8, 8), 8), :]
    for copy in copies:
        copy.wait()

    last = NZ // 2 - 1
    sent = {}

    def hop(way, step, part):
        slot = (z + NZ - step) % NZ if way == 0 else (z + step) % NZ
        copy = pltpu.make_async_remote_copy(
            src_ref=out.at[slot, part],
            dst_ref=out.at[slot, part],
            send_sem=z_send.at[way, step, part],
            recv_sem=z_recv.at[way, step, part],
            device_id=right if way == 0 else left,
            device_id_type=MESH,
        )
        copy.start()
        sent[way, step, part] = copy

    for step in range(NZ // 2):
        for part in range(NX):
            for way in range(2):
                if step:
                    sent[way, step - 1, part].wait_recv()
                if step < last or (part < NX // 2) == (way == 0):
                    hop(way, step, part)
    for (way, step, part), copy in sent.items():
        if step == last:
            copy.wait_recv()
    for copy in sent.values():
        copy.wait_send()


def front(vis, off, gain, st):
    vmem = pl.BlockSpec(memory_space=pltpu.VMEM)
    dma = pltpu.SemaphoreType.DMA
    return pl.pallas_call(
        front_kernel,
        out_shape=jax.ShapeDtypeStruct((NZ, NX, 8, 2048), F32),
        in_specs=[vmem] * 5,
        out_specs=vmem,
        scratch_shapes=[
            pltpu.VMEM((256, 128), F32),
            pltpu.VMEM((8, 32, 128), F32),
            pltpu.VMEM((4, 32, 256), F32),
            pltpu.VMEM((32, 2048), F32),
            pltpu.VMEM((32, 2048), F32),
            dma((NCH - 1,)),
            dma((NCH - 1,)),
            dma((NX - 1,)),
            dma((NX - 1,)),
            dma((2, NZ // 2, NX)),
            dma((2, NZ // 2, NX)),
        ],
        compiler_params=pltpu.CompilerParams(
            collective_id=0, has_side_effects=True, vmem_limit_bytes=40 << 20
        ),
    )(vis, off, gain, st, jnp.asarray(front_table()))


def rows_kernel(places, zat, tiles, wtab, phase, out, lhs, prod, acc):
    step = pl.program_id(0)

    @pl.when(step == 0)
    def _():
        acc[...] = jnp.zeros_like(acc)

    lane = lanes((8, 128))
    low_half = lane < 64

    def one_source(xs, carry):
        for p in range(16):
            v = tiles[0, xs, :, 128 * p : 128 * p + 128]
            high = v.astype(BF).astype(F32)
            rolled = pltpu.roll(v - high, 64, 1)
            first = jnp.concatenate(
                [jnp.where(low_half, high, rolled), jnp.where(low_half, high, 0.0)], 1
            )
            second = jnp.concatenate(
                [jnp.where(low_half, rolled, high), jnp.where(low_half, 0.0, high)], 1
            )
            lhs[16 * p : 16 * p + 16, :] = jnp.concatenate([first, second], 0).astype(BF)
        prod[...] = dot(lhs[...], wtab[0])

        def one_tile(b, carry):
            place = places[(step * NX + xs) * 32 + b]
            tr, tc = place // 32, place % 32
            c = phase[pl.ds(tr, 1), 0:256]
            s = phase[pl.ds(tr, 1), 256:512]
            rows = pl.ds(pl.multiple_of(b * 8, 8), 8)
            for h in range(2):
                re, im = slice(256 * h, 256 * h + 256), slice(512 + 256 * h, 768 + 256 * h)
                pr, pi = prod[rows, re], prod[rows, im]
                acc[tc, :, re] += c * pr - s * pi
                acc[tc, :, im] += c * pi + s * pr
            return carry

        lax.fori_loop(0, 32, one_tile, 0, unroll=4)
        return carry

    lax.fori_loop(0, NX, one_source, 0)

    @pl.when(step == NZ - 1)
    def _():
        for q in range(8):
            prod[32 * q : 32 * q + 32, :] = acc[:, q, :]
        for k in range(8):
            out[128 * k : 128 * k + 128, :] = prod[:, 128 * k : 128 * k + 128].T


def image_rows(places, zat, tiles):
    return pl.pallas_call(
        rows_kernel,
        out_shape=jax.ShapeDtypeStruct((1024, 256), F32),
        grid_spec=pltpu.PrefetchScalarGridSpec(
            num_scalar_prefetch=2,
            grid=(NZ,),
            in_specs=[
                pl.BlockSpec((1, NX, 8, 2048), lambda i, p, z: (i, 0, 0, 0)),
                pl.BlockSpec((1, 256, 1024), lambda i, p, z: (z[0], 0, 0)),
                pl.BlockSpec((256, 512), lambda i, p, z: (0, 0)),
            ],
            out_specs=pl.BlockSpec((1024, 256), lambda i, p, z: (0, 0)),
            scratch_shapes=[
                pltpu.VMEM((256, 256), BF),
                pltpu.VMEM((256, 1024), F32),
                pltpu.VMEM((32, 8, 1024), F32),
            ],
        ),
        compiler_params=pltpu.CompilerParams(vmem_limit_bytes=40 << 20),
    )(places, zat, tiles, jnp.asarray(row_table()), jnp.asarray(row_phase()))


def spread_kernel(rows, out, local, send, recv):
    bt, ch = lax.axis_index("bt"), lax.axis_index("ch")
    z, x = bt // NX, bt % NX
    me = x * NCH + ch
    n = NX * NCH
    barrier = pltpu.get_barrier_semaphore()
    ids = [(me + d) % n for d in range(1, n)]
    peers = [(z * NX + i // NCH, i % NCH) for i in ids]
    for peer in peers:
        pl.semaphore_signal(barrier, inc=1, device_id=peer, device_id_type=MESH)
    own = pltpu.make_async_copy(rows.at[:, me], out.at[me], local)
    own.start()
    pl.semaphore_wait(barrier, n - 1)
    copies = []
    for d, (i, peer) in enumerate(zip(ids, peers)):
        copy = pltpu.make_async_remote_copy(
            src_ref=rows.at[:, i],
            dst_ref=out.at[me],
            send_sem=send.at[d],
            recv_sem=recv.at[d],
            device_id=peer,
            device_id_type=MESH,
        )
        copy.start()
        copies.append(copy)
    for copy in copies:
        copy.wait()
    own.wait()


def spread(rows):
    vmem = pl.BlockSpec(memory_space=pltpu.VMEM)
    n = NX * NCH
    return pl.pallas_call(
        spread_kernel,
        out_shape=jax.ShapeDtypeStruct((n, 2, 16, 256), F32),
        in_specs=[vmem],
        out_specs=vmem,
        scratch_shapes=[
            pltpu.SemaphoreType.DMA,
            pltpu.SemaphoreType.DMA((n - 1,)),
            pltpu.SemaphoreType.DMA((n - 1,)),
        ],
        compiler_params=pltpu.CompilerParams(
            collective_id=1, has_side_effects=True, vmem_limit_bytes=40 << 20
        ),
    )(rows)


def turn(values):
    n = len(values)
    if n == 1:
        return values
    even, odd = turn(values[0::2]), turn(values[1::2])
    low, high = [], []
    for k in range(n // 2):
        er, ei = even[k]
        xr, xi = odd[k]
        if k == 0:
            tr, ti = xr, xi
        elif 4 * k == n:
            tr, ti = -xi, xr
        else:
            c, s = math.cos(2 * math.pi * k / n), math.sin(2 * math.pi * k / n)
            tr, ti = c * xr - s * xi, c * xi + s * xr
        low.append((er + tr, ei + ti))
        high.append((er - tr, ei - ti))
    return low + high


def columns_kernel(parts, whigh, wlow, twiddle, out, vhigh, vlow, mid):
    lane = lanes((16, 128))

    def one_x(x, carry):
        for r in range(2):
            for h in range(2):
                for j in range(2):
                    pieces = [parts[x * 8 + 4 * h + i, r, :, 128 * j : 128 * j + 128] for i in range(4)]
                    for jj in range(4):
                        got = None
                        for i in range(4):
                            shift = (32 * (i - jj)) % 128
                            piece = pltpu.roll(pieces[i], shift, 1) if shift else pieces[i]
                            got = piece if got is None else jnp.where(lane >= 32 * i, piece, got)
                        high, low = halves(got)
                        rows = pl.ds(pl.multiple_of((x * 8 + 4 * j + jj) * 16, 16), 16)
                        at = slice(256 * r + 128 * h, 256 * r + 128 * h + 128)
                        vhigh[rows, at] = high
                        vlow[rows, at] = low
        return carry

    lax.fori_loop(0, NX, one_x, 0)
    mid[...] = dot(vhigh[...], whigh[...]) + (dot(vlow[...], whigh[...]) + dot(vhigh[...], wlow[...]))
    for a in range(2):
        for e in range(2):
            values = []
            for q in range(SUB):
                rows = slice(16 * q + 8 * a, 16 * q + 8 * a + 8)
                zr = mid[rows, 128 * e : 128 * e + 128]
                zi = mid[rows, 256 + 128 * e : 384 + 128 * e]
                c = twiddle[q : q + 1, 128 * e : 128 * e + 128]
                s = twiddle[q : q + 1, 256 + 128 * e : 384 + 128 * e]
                values.append((c * zr - s * zi, c * zi + s * zr))
            for k, (re, im) in enumerate(turn(values)):
                at = slice(256 * k + 128 * e, 256 * k + 128 * e + 128)
                out[0, 8 * a : 8 * a + 8, at] = re
                out[1, 8 * a : 8 * a + 8, at] = im


def columns(parts):
    vmem = pl.BlockSpec(memory_space=pltpu.VMEM)
    high, low = column_table()
    return pl.pallas_call(
        columns_kernel,
        out_shape=jax.ShapeDtypeStruct((2, 16, G), F32),
        in_specs=[vmem] * 4,
        out_specs=vmem,
        scratch_shapes=[
            pltpu.VMEM((512, 512), BF),
            pltpu.VMEM((512, 512), BF),
            pltpu.VMEM((512, 512), F32),
        ],
        compiler_params=pltpu.CompilerParams(vmem_limit_bytes=40 << 20),
    )(parts, jnp.asarray(high), jnp.asarray(low), jnp.asarray(column_twiddle()))


def shards(visibility, cell_offset, station_gain, stations, row_band, tile_offset):
    ch = lax.axis_index("ch")
    zat = (lax.axis_index("bt") // NX).astype(jnp.int32).reshape(1)
    place = (row_band.reshape(-1) * 128 + tile_offset).reshape(NZ * NX, NCH, 32)
    place = lax.dynamic_index_in_dim(place, ch, 1, keepdims=False).reshape(-1)
    tiles = front(visibility, cell_offset, station_gain.reshape(16, 512), stations.T)
    rows = image_rows(place, zat, tiles)
    parts = spread(rows.reshape(2, NX * NCH, 16, 256))
    return columns(parts)


def solution(mesh):
    return jax.shard_map(
        shards,
        mesh=mesh,
        in_specs=(
            P(None, None, "ch", "bt"),
            P(None, None, "ch", "bt"),
            P(None, "ch", None),
            P("bt", None),
            P(),
            P(),
        ),
        out_specs=P(None, ("bt", "ch"), None),
        check_vma=False,
    )
```

```python
import math

import jax
import jax.numpy as jnp
import numpy as np
from jax import lax
from jax.experimental import pallas as pl
from jax.experimental.pallas import tpu as pltpu
from jax.sharding import PartitionSpec as P

MESH = pl.DeviceIdType.MESH
NZ, NX, NCH = 16, 4, 8
SUB = 32
G = 8192
SPAN = G // NZ
BF = jnp.bfloat16
F32 = jnp.float32


def taper_dft():
    half = SUB // 2
    pos = np.concatenate([np.arange(half, SUB), [0], np.arange(half - 1, 0, -1)])
    x = (pos - half) / SUB
    return np.exp(-2j * np.pi * np.outer(np.arange(SUB), x)) * (np.exp(-4.0 * x * x) / math.sqrt(SUB))[None, :]


def front_table():
    table = taper_dft()
    return np.concatenate([table.real, table.imag], 0).astype(np.float32)


def row_table():
    a = np.arange(G)
    u = np.exp(2j * np.pi * np.outer(a, np.arange(SUB)) / G) @ taper_dft()
    u = u.reshape(NZ, SPAN, SUB).transpose(0, 2, 1)
    w = np.concatenate(
        [np.concatenate([u.real, u.imag], 2), np.concatenate([-u.imag, u.real], 2)], 1
    )
    return w.astype(np.float32)


def column_table():
    ang = 2 * np.pi * (np.outer(np.arange(256), np.arange(256)) % 256) / 256
    return np.concatenate([np.cos(ang), np.sin(ang)], 1).astype(np.float32)


def column_twiddle():
    ang = 2 * np.pi * np.outer(np.arange(SUB), np.arange(256)) / G
    scale = 1.0 / (G * 16.0)
    return (np.concatenate([np.cos(ang), np.sin(ang)], 1) * scale).astype(np.float32)


def trig_coefficients():
    f = 0.5 * np.cos(np.pi * (np.arange(4000) + 0.5) / 4000)
    y = f * f
    cosine = np.polynomial.chebyshev.Chebyshev.fit(y, np.cos(2 * np.pi * f), 7, domain=[0, 0.25])
    sine = np.polynomial.chebyshev.Chebyshev.fit(
        y, np.sin(2 * np.pi * f) / f, 6, domain=[0, 0.25]
    )
    convert = np.polynomial.Polynomial
    return (
        [float(v) for v in cosine.convert(kind=convert).coef],
        [float(v) for v in sine.convert(kind=convert).coef],
    )


COS_C, SIN_C = trig_coefficients()


def horner(coefs, y):
    total = jnp.full_like(y, coefs[-1])
    for value in coefs[-2::-1]:
        total = total * y + value
    return total


def phasor(turns):
    f = turns - jnp.floor(turns + 0.5)
    y = f * f
    return horner(COS_C, y), f * horner(SIN_C, y)


def steps(row, u):
    c, s = phasor(row * u)
    end_c = c[8:9] * c[8:9] - s[8:9] * s[8:9]
    end_s = -2.0 * c[8:9] * s[8:9]
    first = lax.broadcasted_iota(jnp.int32, c.shape, 0) == 0
    return (
        jnp.concatenate([c, jnp.where(first, end_c, c)], 0),
        jnp.concatenate([s, jnp.where(first, end_s, -s)], 0),
    )


def halves(v):
    high = v.astype(BF)
    return high, (v - high.astype(F32)).astype(BF)


def dot(a, b, dims=((1,), (0,))):
    return lax.dot_general(a, b, (dims, ((), ())), preferred_element_type=F32)


def lanes(shape):
    return lax.broadcasted_iota(jnp.int32, shape, 1)


def front_kernel(
    vis_hbm, off_hbm, gain_hbm, st_hbm, band_hbm, place_hbm, ttab_hbm, tiles, where_out,
    vis, off, gain, st, band, place, ttab,
    packed, landed, quant, image, tile,
    load, keep, ch_send, ch_recv, x_send, x_recv, z_send, z_recv,
):
    bt, ch = lax.axis_index("bt"), lax.axis_index("ch")
    z, x = bt // NX, bt % NX
    ch_peer = [(bt, (ch + d) % NCH) for d in range(1, NCH)]
    x_peer = [(z * NX + (x + d) % NX, ch) for d in range(1, NX)]
    right = (((z + 1) % NZ) * NX + x, ch)
    left = (((z + NZ - 1) % NZ) * NX + x, ch)
    barrier = pltpu.get_barrier_semaphore()
    peers = ch_peer + x_peer + [right, left]
    for peer in peers:
        pl.semaphore_signal(barrier, inc=1, device_id=peer, device_id_type=MESH)
    loads = [
        pltpu.make_async_copy(src, dst, load.at[i])
        for i, (src, dst) in enumerate(
            [
                (gain_hbm, gain), (st_hbm, st), (vis_hbm, vis), (off_hbm, off), (band_hbm, band),
                (place_hbm, place), (ttab_hbm, ttab),
            ]
        )
    ]
    for copy in loads:
        copy.start()

    loads[0].wait()
    loads[1].wait()
    g = gain[...]
    g0 = g.astype(BF)
    rest = g - g0.astype(F32)
    g1 = rest.astype(BF)
    g2 = (rest - g1.astype(F32)).astype(BF)
    parts = jnp.concatenate([g0, g1, g2], 0)
    stations = lax.broadcasted_iota(jnp.int32, (512, 256), 0)

    def pick(row):
        hot = jnp.where(stations == st[row : row + 1, :], 1.0, 0.0).astype(BF)
        got = dot(parts, hot)
        got = (got[0:16] + got[16:32]) + got[32:48]
        return got[0:8], got[8:16]

    pr, pi = pick(0)
    qr, qi = pick(1)
    ar = pr * qr + pi * qi
    ai = pi * qr - pr * qi
    loads[2].wait()
    loads[3].wait()
    rows_r, rows_i, rows_u, rows_v = [], [], [], []
    for t in range(4):
        vr, vi = vis[0, t], vis[1, t]
        rows_r.append(vr * ar - vi * ai)
        rows_i.append(vr * ai + vi * ar)
        rows_u.append(off[0, t])
        rows_v.append(off[1, t])
    packed[...] = jnp.concatenate(rows_r + rows_i + rows_u + rows_v, 0).T

    pl.semaphore_wait(barrier, len(peers))
    copies = []
    for d, peer in enumerate(ch_peer):
        copy = pltpu.make_async_remote_copy(
            src_ref=packed.at[pl.ds(pl.multiple_of(peer[1] * 32, 32), 32)],
            dst_ref=landed.at[ch],
            send_sem=ch_send.at[d],
            recv_sem=ch_recv.at[d],
            device_id=peer,
            device_id_type=MESH,
        )
        copy.start()
        copies.append(copy)
    landed[ch] = packed[pl.ds(pl.multiple_of(ch * 32, 32), 32), :]

    for copy in loads[4:7]:
        copy.wait()
    lane16 = lanes((NZ, 128))
    where = None
    for xs in range(NX):
        at = pl.ds(2 * xs + ch // 4, NZ, stride=8)
        piece = band[at, :] * 128 + place[at, :]
        piece = pltpu.roll(piece, (32 * xs + 128 - 32 * (ch % 4)) % 128, 1)
        where = piece if where is None else jnp.where(lane16 >= 32 * xs, piece, where)
    where_out[...] = where
    for copy in copies:
        copy.wait()

    lane = lanes((32, 128))
    for h in range(2):
        for q in range(4):
            got = None
            for i in range(4):
                shift = (32 * (i - q)) % 128
                piece = landed[4 * h + i]
                if shift:
                    piece = pltpu.roll(piece, shift, 1)
                got = piece if got is None else jnp.where(lane >= 32 * i, piece, got)
            quant[q, :, 128 * h : 128 * h + 128] = got

    xl = lax.broadcasted_iota(jnp.int32, (16, 256), 0).astype(F32) * (1.0 / 32.0)
    sign = jnp.where((lane // 32) % 2 == 0, -1.0, 1.0)

    def one_block(b):
        wr = quant[0, pl.ds(b, 1), :]
        wi = quant[1, pl.ds(b, 1), :]
        u = quant[2, pl.ds(b, 1), :]
        v = quant[3, pl.ds(b, 1), :]
        cu, su = steps(xl, u)
        rr, ri = steps(xl, v)
        lr = wr * cu - wi * su
        li = wr * su + wi * cu
        lrh, lrl = halves(lr)
        lih, lil = halves(li)
        rrh, rrl = halves(rr)
        rih, ril = halves(ri)
        d = dot(
            jnp.concatenate([rrh, rih, rrl, ril], 0),
            jnp.concatenate([lrh, lih, lrl, lil], 0),
            ((1,), (1,)),
        )
        pr_ = d[0:32] + d[64:96]
        pi_ = d[32:64] + d[96:128]
        pr_ = pr_ + pltpu.roll(pr_, 64, 1)
        pi_ = pi_ + pltpu.roll(pi_, 64, 1)
        return pr_ + sign * pltpu.roll(pi_, 32, 1)

    def x_copy(c, d):
        to = (x + d + 1) % NX
        return pltpu.make_async_remote_copy(
            src_ref=tile.at[c, pl.ds(pl.multiple_of(to * 8, 8), 8)],
            dst_ref=tiles.at[z, c, x],
            send_sem=x_send.at[c, d],
            recv_sem=x_recv.at[c, d],
            device_id=x_peer[d],
            device_id_type=MESH,
        )

    sent = {}

    def hop(way, step, c):
        slot = (z + NZ - step) % NZ if way == 0 else (z + step) % NZ
        copy = pltpu.make_async_remote_copy(
            src_ref=tiles.at[slot, c],
            dst_ref=tiles.at[slot, c],
            send_sem=z_send.at[way, step, c],
            recv_sem=z_recv.at[way, step, c],
            device_id=right if way == 0 else left,
            device_id_type=MESH,
        )
        copy.start()
        sent[way, step, c] = copy

    thigh, tlow = halves(ttab[...])
    tparts = jnp.concatenate([thigh, thigh, tlow], 1)
    crossing = {}

    def leave(c):
        for copy in crossing[c]:
            copy.wait()
        for way in range(2):
            hop(way, 0, c)

    for c in range(4):

        def pair(p, carry):
            b = 8 * c + 2 * p
            both = jnp.where(lane < 64, one_block(b), one_block(b + 1))
            image[:, pl.ds(pl.multiple_of(p * 128, 128), 128)] = both
            return carry

        lax.fori_loop(0, 4, pair, 0, unroll=4)
        high, low = halves(image[...])
        ts = dot(tparts, jnp.concatenate([high, low, high], 0))
        for k in range(4):
            at = slice(128 * k, 128 * k + 128)
            tr, ti = ts[0:32, at], ts[32:64, at]
            other = jnp.where(sign < 0, pltpu.roll(ti, 96, 1), pltpu.roll(ti, 32, 1))
            tile[c, :, at] = tr + sign * other
        crossing[c] = [x_copy(c, d) for d in range(NX - 1)]
        for copy in crossing[c]:
            copy.start()
        own = pltpu.make_async_copy(
            tile.at[c, pl.ds(pl.multiple_of(x * 8, 8), 8)], tiles.at[z, c, x], keep.at[c]
        )
        own.start()
        crossing[c].append(own)
        if c:
            leave(c - 1)
    leave(3)

    last = NZ // 2 - 1
    for step in range(1, NZ // 2):
        for c in range(4):
            for way in range(2):
                sent[way, step - 1, c].wait_recv()
                if step < last or (c < 2) == (way == 0):
                    hop(way, step, c)
    for (way, step, c), copy in sent.items():
        if step == last:
            copy.wait_recv()
    for copy in sent.values():
        copy.wait_send()


def front(vis, off, gain, st, band, place):
    hbm = pl.BlockSpec(memory_space=pl.ANY)
    vmem = pl.BlockSpec(memory_space=pltpu.VMEM)
    dma = pltpu.SemaphoreType.DMA
    return pl.pallas_call(
        front_kernel,
        out_shape=[
            jax.ShapeDtypeStruct((NZ, 4, NX, 8, 512), F32),
            jax.ShapeDtypeStruct((NZ, 128), jnp.int32),
        ],
        in_specs=[hbm] * 7,
        out_specs=[hbm, vmem],
        scratch_shapes=[
            pltpu.VMEM((2, 4, 8, 256), F32),
            pltpu.VMEM((2, 4, 8, 256), F32),
            pltpu.VMEM((16, 512), F32),
            pltpu.VMEM((2, 256), jnp.int32),
            pltpu.VMEM((128, 128), jnp.int32),
            pltpu.VMEM((128, 128), jnp.int32),
            pltpu.VMEM((64, 32), F32),
            pltpu.VMEM((256, 128), F32),
            pltpu.VMEM((8, 32, 128), F32),
            pltpu.VMEM((4, 32, 256), F32),
            pltpu.VMEM((32, 512), F32),
            pltpu.VMEM((4, 32, 512), F32),
            dma((7,)),
            dma((4,)),
            dma((NCH - 1,)),
            dma((NCH - 1,)),
            dma((4, NX - 1)),
            dma((4, NX - 1)),
            dma((2, NZ // 2, 4)),
            dma((2, NZ // 2, 4)),
        ],
        compiler_params=pltpu.CompilerParams(
            collective_id=0, has_side_effects=True, vmem_limit_bytes=58 << 20
        ),
    )(vis, off, gain, st, band, place, jnp.asarray(front_table()))


def rows_kernel(
    tiles_hbm, where, utab_hbm, out,
    tiles, utab, phase, wtab, where_s, lhs, prod_a, prod_b, acc, load, fetch,
):
    z = lax.axis_index("bt") // NX
    loads = [
        pltpu.make_async_copy(utab_hbm.at[z], utab, load.at[0]),
        pltpu.make_async_copy(where, where_s, load.at[1]),
    ]

    def slot_copy(slot):
        return pltpu.make_async_copy(tiles_hbm.at[slot], tiles.at[slot], fetch.at[slot])

    slot_copy(0).start()
    for copy in loads:
        copy.start()
    for slot in range(1, NZ):
        slot_copy(slot).start()
    acc[...] = jnp.zeros_like(acc)
    low_half = lanes((8, 128)) < 64

    def build(slot):
        for c in range(4):
            for xs in range(NX):
                for p in range(4):
                    v = tiles[slot, c, xs, :, 128 * p : 128 * p + 128]
                    high = v.astype(BF).astype(F32)
                    rolled = pltpu.roll(v - high, 64, 1)
                    first = jnp.concatenate(
                        [jnp.where(low_half, high, rolled), jnp.where(low_half, high, 0.0)], 1
                    )
                    second = jnp.concatenate(
                        [jnp.where(low_half, rolled, high), jnp.where(low_half, 0.0, high)], 1
                    )
                    k = 256 * c + 64 * xs + 16 * p
                    lhs[k : k + 16, :] = jnp.concatenate([first, second], 0).astype(BF)

    def add_tile(slot, prod, c, b):
        word = where_s[slot, (b // 8) * 32 + c * 8 + b % 8]
        tr, tc = word >> 5, word & 31
        cs, sn = phase[pl.ds(tr, 1), 0:256], phase[pl.ds(tr, 1), 256:512]
        rows = pl.ds(pl.multiple_of(c * 256 + 8 * b, 8), 8)
        for h in range(2):
            re, im = slice(256 * h, 256 * h + 256), slice(512 + 256 * h, 768 + 256 * h)
            pr, pi = prod[rows, re], prod[rows, im]
            acc[tc, :, re] += cs * pr - sn * pi
            acc[tc, :, im] += cs * pi + sn * pr

    for k in range(4):
        tr = lax.broadcasted_iota(jnp.int32, (64, 256), 0) + 64 * k
        turns = (tr * lanes((64, 256)) % 256).astype(F32) * (1.0 / 256.0)
        phase[64 * k : 64 * k + 64, 0:256], phase[64 * k : 64 * k + 64, 256:512] = phasor(turns)
    slot_copy(0).wait()
    build(0)
    for copy in loads:
        copy.wait()
    uhigh, ulow = halves(utab[...])
    wtab[...] = jnp.concatenate([uhigh, uhigh, ulow, ulow], 0)
    prod_a[...] = dot(lhs[...], wtab[...])

    def two(m, carry):
        for slot, now, later in ((2 * m, prod_a, prod_b), (2 * m + 1, prod_b, prod_a)):
            following = jnp.minimum(slot + 1, NZ - 1)

            @pl.when(slot + 1 < NZ)
            def _():
                slot_copy(following).wait()

            build(following)

            def part(c, carry):
                at = pl.ds(pl.multiple_of(256 * c, 256), 256)
                later[:, at] = dot(lhs[...], wtab[:, at])
                for b in range(32):
                    add_tile(slot, now, c, b)
                return carry

            lax.fori_loop(0, 4, part, 0)
        return carry

    lax.fori_loop(0, NZ // 2, two, 0)

    for q in range(8):
        prod_a[32 * q : 32 * q + 32, :] = acc[:, q, :]
    for k in range(8):
        out[128 * k : 128 * k + 128, :] = prod_a[0:256, 128 * k : 128 * k + 128].T


def image_rows(tiles, where):
    hbm = pl.BlockSpec(memory_space=pl.ANY)
    vmem = pl.BlockSpec(memory_space=pltpu.VMEM)
    return pl.pallas_call(
        rows_kernel,
        out_shape=jax.ShapeDtypeStruct((1024, 256), F32),
        in_specs=[hbm] * 3,
        out_specs=vmem,
        scratch_shapes=[
            pltpu.VMEM((NZ, 4, NX, 8, 512), F32),
            pltpu.VMEM((64, 1024), F32),
            pltpu.VMEM((256, 512), F32),
            pltpu.VMEM((256, 1024), BF),
            pltpu.SMEM((NZ, 128), jnp.int32),
            pltpu.VMEM((1024, 256), BF),
            pltpu.VMEM((1024, 1024), F32),
            pltpu.VMEM((1024, 1024), F32),
            pltpu.VMEM((32, 8, 1024), F32),
            pltpu.SemaphoreType.DMA((2,)),
            pltpu.SemaphoreType.DMA((NZ,)),
        ],
        compiler_params=pltpu.CompilerParams(vmem_limit_bytes=52 << 20),
    )(tiles, where, jnp.asarray(row_table()))


def spread_kernel(rows, out, stage, local, send, recv, there, here, onward, landed):
    bt, ch = lax.axis_index("bt"), lax.axis_index("ch")
    z, x = bt // NX, bt % NX
    y, core = ch // 2, ch % 2
    me = x * NCH + ch

    def at(dx, dy, dc):
        xx, yy, cc = (x + dx) % NX, (y + dy) % 4, (core + dc) % 2
        return xx * NCH + 2 * yy + cc, (z * NX + xx, 2 * yy + cc)

    steps = [(dx, dy, dc) for dx in (2, 1, 3, 0) for dy in (2, 1, 3, 0) for dc in (0, 1)][:-2] + [(0, 0, 1)]
    around = [((2, dy, 1), (3, 0, 0), (1, 0, 0), (3, dy, 1)) for dy in range(4)]
    around += [((dx, 2, 0), (0, 3, 0), (0, 1, 0), (dx, 3, 0)) for dx in range(4)]
    straight = [step for step in steps if step not in [way[0] for way in around]]
    barrier = pltpu.get_barrier_semaphore()
    for step in steps:
        pl.semaphore_signal(barrier, inc=1, device_id=at(*step)[1], device_id_type=MESH)
    own = pltpu.make_async_copy(rows.at[:, me], out.at[me], local)
    own.start()
    pl.semaphore_wait(barrier, len(steps))

    def remote(src, dst, sender, receiver, peer):
        copy = pltpu.make_async_remote_copy(
            src_ref=src,
            dst_ref=dst,
            send_sem=sender,
            recv_sem=receiver,
            device_id=peer,
            device_id_type=MESH,
        )
        copy.start()
        return copy

    first = [
        remote(rows.at[:, at(*goal)[0]], stage.at[j], there.at[j], here.at[j], at(*relay)[1])
        for j, (goal, relay, _, _) in enumerate(around)
    ]
    copies = [
        remote(rows.at[:, at(*goal)[0]], out.at[me], send.at[j], recv.at[j], at(*goal)[1])
        for j, goal in enumerate(straight)
    ]
    for j, (_, _, origin, goal) in enumerate(around):
        first[j].wait_recv()
        copies.append(
            remote(stage.at[j], out.at[at(*origin)[0]], onward.at[j], landed.at[j], at(*goal)[1])
        )
    for copy in copies:
        copy.wait()
    for copy in first:
        copy.wait_send()
    own.wait()


def spread(rows):
    vmem = pl.BlockSpec(memory_space=pltpu.VMEM)
    n = NX * NCH
    dma = pltpu.SemaphoreType.DMA
    return pl.pallas_call(
        spread_kernel,
        out_shape=jax.ShapeDtypeStruct((n, 2, 16, 256), F32),
        in_specs=[vmem],
        out_specs=vmem,
        scratch_shapes=[
            pltpu.VMEM((8, 2, 16, 256), F32),
            dma,
            dma((n - 9,)),
            dma((n - 9,)),
            dma((8,)),
            dma((8,)),
            dma((8,)),
            dma((8,)),
        ],
        compiler_params=pltpu.CompilerParams(
            collective_id=1, has_side_effects=True, vmem_limit_bytes=40 << 20
        ),
    )(rows)


def turn(values):
    n = len(values)
    if n == 1:
        return values
    even, odd = turn(values[0::2]), turn(values[1::2])
    low, high = [], []
    for k in range(n // 2):
        er, ei = even[k]
        xr, xi = odd[k]
        if k == 0:
            tr, ti = xr, xi
        elif 4 * k == n:
            tr, ti = -xi, xr
        else:
            c, s = math.cos(2 * math.pi * k / n), math.sin(2 * math.pi * k / n)
            tr, ti = c * xr - s * xi, c * xi + s * xr
        low.append((er + tr, ei + ti))
        high.append((er - tr, ei - ti))
    return low + high


def columns_kernel(parts, table, twiddle, out, whigh, wlow, vhigh, vlow, mid):
    c, s = table[:, 0:256], table[:, 256:512]
    for rows, both in ((slice(0, 256), table[...]), (slice(256, 512), jnp.concatenate([-s, c], 1))):
        whigh[rows, :], wlow[rows, :] = halves(both)
    lane = lanes((16, 128))

    def one_x(x, carry):
        for r in range(2):
            for h in range(2):
                for j in range(2):
                    pieces = [parts[x * 8 + 4 * h + i, r, :, 128 * j : 128 * j + 128] for i in range(4)]
                    for jj in range(4):
                        got = None
                        for i in range(4):
                            shift = (32 * (i - jj)) % 128
                            piece = pltpu.roll(pieces[i], shift, 1) if shift else pieces[i]
                            got = piece if got is None else jnp.where(lane >= 32 * i, piece, got)
                        high, low = halves(got)
                        rows = pl.ds(pl.multiple_of((x * 8 + 4 * j + jj) * 16, 16), 16)
                        at = slice(256 * r + 128 * h, 256 * r + 128 * h + 128)
                        vhigh[rows, at] = high
                        vlow[rows, at] = low
        return carry

    lax.fori_loop(0, NX, one_x, 0)
    mid[...] = dot(vhigh[...], whigh[...]) + (dot(vlow[...], whigh[...]) + dot(vhigh[...], wlow[...]))
    for a in range(2):
        for e in range(2):
            values = []
            for q in range(SUB):
                rows = slice(16 * q + 8 * a, 16 * q + 8 * a + 8)
                zr = mid[rows, 128 * e : 128 * e + 128]
                zi = mid[rows, 256 + 128 * e : 384 + 128 * e]
                c = twiddle[q : q + 1, 128 * e : 128 * e + 128]
                s = twiddle[q : q + 1, 256 + 128 * e : 384 + 128 * e]
                values.append((c * zr - s * zi, c * zi + s * zr))
            for k, (re, im) in enumerate(turn(values)):
                at = slice(256 * k + 128 * e, 256 * k + 128 * e + 128)
                out[0, 8 * a : 8 * a + 8, at] = re
                out[1, 8 * a : 8 * a + 8, at] = im


def columns(parts):
    vmem = pl.BlockSpec(memory_space=pltpu.VMEM)
    return pl.pallas_call(
        columns_kernel,
        out_shape=jax.ShapeDtypeStruct((2, 16, G), F32),
        in_specs=[vmem] * 3,
        out_specs=vmem,
        scratch_shapes=[
            pltpu.VMEM((512, 512), BF),
            pltpu.VMEM((512, 512), BF),
            pltpu.VMEM((512, 512), BF),
            pltpu.VMEM((512, 512), BF),
            pltpu.VMEM((512, 512), F32),
        ],
        compiler_params=pltpu.CompilerParams(vmem_limit_bytes=40 << 20),
    )(parts, jnp.asarray(column_table()), jnp.asarray(column_twiddle()))


def shards(visibility, cell_offset, station_gain, stations, row_band, tile_offset):
    tiles, where = front(
        visibility,
        cell_offset,
        station_gain.reshape(16, 512),
        stations.T,
        row_band.reshape(128, 128),
        tile_offset.reshape(128, 128),
    )
    rows = image_rows(tiles, where)
    return columns(spread(rows.reshape(2, NX * NCH, 16, 256)))


def solution(mesh):
    return jax.shard_map(
        shards,
        mesh=mesh,
        in_specs=(
            P(None, None, "ch", "bt"),
            P(None, None, "ch", "bt"),
            P(None, "ch", None),
            P("bt", None),
            P(),
            P(),
        ),
        out_specs=P(None, ("bt", "ch"), None),
        check_vma=False,
    )
```

```python
import math

import jax
import jax.numpy as jnp
import numpy as np
from jax import lax
from jax.experimental import pallas as pl
from jax.experimental.pallas import tpu as pltpu
from jax.sharding import PartitionSpec as P

MESH = pl.DeviceIdType.MESH
NZ, NX, NCH = 16, 4, 8
SUB = 32
G = 8192
SPAN = G // NZ
BF = jnp.bfloat16
F32 = jnp.float32


def taper_dft():
    half = SUB // 2
    pos = np.concatenate([np.arange(half, SUB), [0], np.arange(half - 1, 0, -1)])
    x = (pos - half) / SUB
    return np.exp(-2j * np.pi * np.outer(np.arange(SUB), x)) * (np.exp(-4.0 * x * x) / math.sqrt(SUB))[None, :]


def front_table():
    table = taper_dft()
    return np.concatenate([table.real, table.imag], 0).astype(np.float32)


def row_table():
    a = np.arange(G)
    u = np.exp(2j * np.pi * np.outer(a, np.arange(SUB)) / G) @ taper_dft()
    u = u.reshape(NZ, SPAN, SUB).transpose(0, 2, 1)
    w = np.concatenate(
        [np.concatenate([u.real, u.imag], 2), np.concatenate([-u.imag, u.real], 2)], 1
    )
    return w.astype(np.float32)


def column_table():
    ang = 2 * np.pi * (np.outer(np.arange(256), np.arange(256)) % 256) / 256
    return np.concatenate([np.cos(ang), np.sin(ang)], 1).astype(np.float32)


def column_twiddle():
    ang = 2 * np.pi * np.outer(np.arange(SUB), np.arange(256)) / G
    scale = 1.0 / (G * 16.0)
    return (np.concatenate([np.cos(ang), np.sin(ang)], 1) * scale).astype(np.float32)


def trig_coefficients():
    f = 0.5 * np.cos(np.pi * (np.arange(4000) + 0.5) / 4000)
    y = f * f
    cosine = np.polynomial.chebyshev.Chebyshev.fit(y, np.cos(2 * np.pi * f), 7, domain=[0, 0.25])
    sine = np.polynomial.chebyshev.Chebyshev.fit(
        y, np.sin(2 * np.pi * f) / f, 6, domain=[0, 0.25]
    )
    convert = np.polynomial.Polynomial
    return (
        [float(v) for v in cosine.convert(kind=convert).coef],
        [float(v) for v in sine.convert(kind=convert).coef],
    )


COS_C, SIN_C = trig_coefficients()


def horner(coefs, y):
    total = jnp.full_like(y, coefs[-1])
    for value in coefs[-2::-1]:
        total = total * y + value
    return total


def phasor(turns):
    f = turns - jnp.floor(turns + 0.5)
    y = f * f
    return horner(COS_C, y), f * horner(SIN_C, y)


def steps(row, u):
    c, s = phasor(row * u)
    end_c = c[8:9] * c[8:9] - s[8:9] * s[8:9]
    end_s = -2.0 * c[8:9] * s[8:9]
    first = lax.broadcasted_iota(jnp.int32, c.shape, 0) == 0
    return (
        jnp.concatenate([c, jnp.where(first, end_c, c)], 0),
        jnp.concatenate([s, jnp.where(first, end_s, -s)], 0),
    )


def halves(v):
    high = v.astype(BF)
    return high, (v - high.astype(F32)).astype(BF)


def dot(a, b, dims=((1,), (0,))):
    return lax.dot_general(a, b, (dims, ((), ())), preferred_element_type=F32)


def lanes(shape):
    return lax.broadcasted_iota(jnp.int32, shape, 1)


def front_kernel(
    vis_hbm, off_hbm, gain_hbm, st_hbm, band_hbm, place_hbm, ttab_hbm, tiles, where_out,
    vis, off, gain, st, band, place, ttab,
    packed, landed, quant, image, tile,
    load, keep, ch_send, ch_recv, x_send, x_recv, z_send, z_recv,
):
    bt, ch = lax.axis_index("bt"), lax.axis_index("ch")
    z, x = bt // NX, bt % NX
    ch_peer = [(bt, (ch + d) % NCH) for d in range(1, NCH)]
    x_peer = [(z * NX + (x + d) % NX, ch) for d in range(1, NX)]
    right = (((z + 1) % NZ) * NX + x, ch)
    left = (((z + NZ - 1) % NZ) * NX + x, ch)
    barrier = pltpu.get_barrier_semaphore()
    peers = ch_peer + x_peer + [right, left]
    for peer in peers:
        pl.semaphore_signal(barrier, inc=1, device_id=peer, device_id_type=MESH)
    loads = [
        pltpu.make_async_copy(src, dst, load.at[i])
        for i, (src, dst) in enumerate(
            [
                (gain_hbm, gain), (st_hbm, st), (vis_hbm, vis), (off_hbm, off), (band_hbm, band),
                (place_hbm, place), (ttab_hbm, ttab),
            ]
        )
    ]
    for copy in loads:
        copy.start()

    loads[0].wait()
    loads[1].wait()
    g = gain[...]
    g0 = g.astype(BF)
    rest = g - g0.astype(F32)
    g1 = rest.astype(BF)
    g2 = (rest - g1.astype(F32)).astype(BF)
    parts = jnp.concatenate([g0, g1, g2], 0)
    stations = lax.broadcasted_iota(jnp.int32, (512, 256), 0)

    def pick(row):
        hot = jnp.where(stations == st[row : row + 1, :], 1.0, 0.0).astype(BF)
        got = dot(parts, hot)
        got = (got[0:16] + got[16:32]) + got[32:48]
        return got[0:8], got[8:16]

    pr, pi = pick(0)
    qr, qi = pick(1)
    ar = pr * qr + pi * qi
    ai = pi * qr - pr * qi
    loads[2].wait()
    loads[3].wait()
    rows_r, rows_i, rows_u, rows_v = [], [], [], []
    for t in range(4):
        vr, vi = vis[0, t], vis[1, t]
        rows_r.append(vr * ar - vi * ai)
        rows_i.append(vr * ai + vi * ar)
        rows_u.append(off[0, t])
        rows_v.append(off[1, t])
    packed[...] = jnp.concatenate(rows_r + rows_i + rows_u + rows_v, 0).T

    pl.semaphore_wait(barrier, len(peers))
    copies = []
    for d, peer in enumerate(ch_peer):
        copy = pltpu.make_async_remote_copy(
            src_ref=packed.at[pl.ds(pl.multiple_of(peer[1] * 32, 32), 32)],
            dst_ref=landed.at[ch],
            send_sem=ch_send.at[d],
            recv_sem=ch_recv.at[d],
            device_id=peer,
            device_id_type=MESH,
        )
        copy.start()
        copies.append(copy)
    landed[ch] = packed[pl.ds(pl.multiple_of(ch * 32, 32), 32), :]

    for copy in loads[4:7]:
        copy.wait()
    lane16 = lanes((NZ, 128))
    where = None
    for xs in range(NX):
        at = pl.ds(2 * xs + ch // 4, NZ, stride=8)
        piece = band[at, :] * 128 + place[at, :]
        piece = pltpu.roll(piece, (32 * xs + 128 - 32 * (ch % 4)) % 128, 1)
        where = piece if where is None else jnp.where(lane16 >= 32 * xs, piece, where)
    where_out[...] = where
    for copy in copies:
        copy.wait()

    lane = lanes((32, 128))
    for h in range(2):
        for q in range(4):
            got = None
            for i in range(4):
                shift = (32 * (i - q)) % 128
                piece = landed[4 * h + i]
                if shift:
                    piece = pltpu.roll(piece, shift, 1)
                got = piece if got is None else jnp.where(lane >= 32 * i, piece, got)
            quant[q, :, 128 * h : 128 * h + 128] = got

    xl = lax.broadcasted_iota(jnp.int32, (16, 256), 0).astype(F32) * (1.0 / 32.0)
    sign = jnp.where((lane // 32) % 2 == 0, -1.0, 1.0)

    def one_block(b):
        wr = quant[0, pl.ds(b, 1), :]
        wi = quant[1, pl.ds(b, 1), :]
        u = quant[2, pl.ds(b, 1), :]
        v = quant[3, pl.ds(b, 1), :]
        cu, su = steps(xl, u)
        rr, ri = steps(xl, v)
        lr = wr * cu - wi * su
        li = wr * su + wi * cu
        lrh, lrl = halves(lr)
        lih, lil = halves(li)
        rrh, rrl = halves(rr)
        rih, ril = halves(ri)
        d = dot(
            jnp.concatenate([rrh, rih, rrl, ril], 0),
            jnp.concatenate([lrh, lih, lrl, lil], 0),
            ((1,), (1,)),
        )
        pr_ = d[0:32] + d[64:96]
        pi_ = d[32:64] + d[96:128]
        pr_ = pr_ + pltpu.roll(pr_, 64, 1)
        pi_ = pi_ + pltpu.roll(pi_, 64, 1)
        return pr_ + sign * pltpu.roll(pi_, 32, 1)

    def x_copy(c, d):
        to = (x + d + 1) % NX
        return pltpu.make_async_remote_copy(
            src_ref=tile.at[c, pl.ds(pl.multiple_of(to * 8, 8), 8)],
            dst_ref=tiles.at[z, c, x],
            send_sem=x_send.at[c, d],
            recv_sem=x_recv.at[c, d],
            device_id=x_peer[d],
            device_id_type=MESH,
        )

    sent = {}

    def hop(way, step, c):
        slot = (z + NZ - step) % NZ if way == 0 else (z + step) % NZ
        copy = pltpu.make_async_remote_copy(
            src_ref=tiles.at[slot, c],
            dst_ref=tiles.at[slot, c],
            send_sem=z_send.at[way, step, c],
            recv_sem=z_recv.at[way, step, c],
            device_id=right if way == 0 else left,
            device_id_type=MESH,
        )
        copy.start()
        sent[way, step, c] = copy

    thigh, tlow = halves(ttab[...])
    tparts = jnp.concatenate([thigh, thigh, tlow], 1)
    crossing = {}

    def leave(c):
        for copy in crossing[c]:
            copy.wait()
        for way in range(2):
            hop(way, 0, c)

    for c in range(4):

        def pair(p, carry):
            b = 8 * c + 2 * p
            both = jnp.where(lane < 64, one_block(b), one_block(b + 1))
            image[:, pl.ds(pl.multiple_of(p * 128, 128), 128)] = both
            return carry

        lax.fori_loop(0, 4, pair, 0, unroll=4)
        high, low = halves(image[...])
        ts = dot(tparts, jnp.concatenate([high, low, high], 0))
        for k in range(4):
            at = slice(128 * k, 128 * k + 128)
            tr, ti = ts[0:32, at], ts[32:64, at]
            other = jnp.where(sign < 0, pltpu.roll(ti, 96, 1), pltpu.roll(ti, 32, 1))
            tile[c, :, at] = tr + sign * other
        crossing[c] = [x_copy(c, d) for d in range(NX - 1)]
        for copy in crossing[c]:
            copy.start()
        own = pltpu.make_async_copy(
            tile.at[c, pl.ds(pl.multiple_of(x * 8, 8), 8)], tiles.at[z, c, x], keep.at[c]
        )
        own.start()
        crossing[c].append(own)
        if c:
            leave(c - 1)
    leave(3)

    last = NZ // 2 - 1
    for step in range(1, NZ // 2):
        for c in range(4):
            for way in range(2):
                sent[way, step - 1, c].wait_recv()
                if step < last or (c < 2) == (way == 0):
                    hop(way, step, c)
    for (way, step, c), copy in sent.items():
        if step == last:
            copy.wait_recv()
    for copy in sent.values():
        copy.wait_send()


def front(vis, off, gain, st, band, place):
    hbm = pl.BlockSpec(memory_space=pl.ANY)
    vmem = pl.BlockSpec(memory_space=pltpu.VMEM)
    dma = pltpu.SemaphoreType.DMA
    return pl.pallas_call(
        front_kernel,
        out_shape=[
            jax.ShapeDtypeStruct((NZ, 4, NX, 8, 512), F32),
            jax.ShapeDtypeStruct((NZ, 128), jnp.int32),
        ],
        in_specs=[hbm] * 7,
        out_specs=[hbm, vmem],
        scratch_shapes=[
            pltpu.VMEM((2, 4, 8, 256), F32),
            pltpu.VMEM((2, 4, 8, 256), F32),
            pltpu.VMEM((16, 512), F32),
            pltpu.VMEM((2, 256), jnp.int32),
            pltpu.VMEM((128, 128), jnp.int32),
            pltpu.VMEM((128, 128), jnp.int32),
            pltpu.VMEM((64, 32), F32),
            pltpu.VMEM((256, 128), F32),
            pltpu.VMEM((8, 32, 128), F32),
            pltpu.VMEM((4, 32, 256), F32),
            pltpu.VMEM((32, 512), F32),
            pltpu.VMEM((4, 32, 512), F32),
            dma((7,)),
            dma((4,)),
            dma((NCH - 1,)),
            dma((NCH - 1,)),
            dma((4, NX - 1)),
            dma((4, NX - 1)),
            dma((2, NZ // 2, 4)),
            dma((2, NZ // 2, 4)),
        ],
        compiler_params=pltpu.CompilerParams(
            collective_id=0, has_side_effects=True, vmem_limit_bytes=58 << 20
        ),
    )(vis, off, gain, st, band, place, jnp.asarray(front_table()))


def rows_kernel(
    tiles_hbm, where, utab_hbm, out,
    tiles, utab, phase, wtab, where_s, lhs, prod_a, prod_b, acc, load, fetch,
):
    z = lax.axis_index("bt") // NX
    loads = [
        pltpu.make_async_copy(utab_hbm.at[z], utab, load.at[0]),
        pltpu.make_async_copy(where, where_s, load.at[1]),
    ]

    def slot_copy(slot):
        return pltpu.make_async_copy(tiles_hbm.at[slot], tiles.at[slot], fetch.at[slot])

    slot_copy(0).start()
    for copy in loads:
        copy.start()
    for slot in range(1, NZ):
        slot_copy(slot).start()
    acc[...] = jnp.zeros_like(acc)
    low_half = lanes((8, 128)) < 64

    def build(slot):
        for c in range(4):
            for xs in range(NX):
                for p in range(4):
                    v = tiles[slot, c, xs, :, 128 * p : 128 * p + 128]
                    high = v.astype(BF).astype(F32)
                    rolled = pltpu.roll(v - high, 64, 1)
                    first = jnp.concatenate(
                        [jnp.where(low_half, high, rolled), jnp.where(low_half, high, 0.0)], 1
                    )
                    second = jnp.concatenate(
                        [jnp.where(low_half, rolled, high), jnp.where(low_half, 0.0, high)], 1
                    )
                    k = 256 * c + 64 * xs + 16 * p
                    lhs[k : k + 16, :] = jnp.concatenate([first, second], 0).astype(BF)

    def add_tile(slot, prod, c, b):
        word = where_s[slot, (b // 8) * 32 + c * 8 + b % 8]
        tr, tc = word >> 5, word & 31
        cs, sn = phase[pl.ds(tr, 1), 0:256], phase[pl.ds(tr, 1), 256:512]
        rows = pl.ds(pl.multiple_of(c * 256 + 8 * b, 8), 8)
        for h in range(2):
            re, im = slice(256 * h, 256 * h + 256), slice(512 + 256 * h, 768 + 256 * h)
            pr, pi = prod[rows, re], prod[rows, im]
            acc[tc, :, re] += cs * pr - sn * pi
            acc[tc, :, im] += cs * pi + sn * pr

    for k in range(4):
        tr = lax.broadcasted_iota(jnp.int32, (64, 256), 0) + 64 * k
        turns = (tr * lanes((64, 256)) % 256).astype(F32) * (1.0 / 256.0)
        phase[64 * k : 64 * k + 64, 0:256], phase[64 * k : 64 * k + 64, 256:512] = phasor(turns)
    slot_copy(0).wait()
    build(0)
    for copy in loads:
        copy.wait()
    uhigh, ulow = halves(utab[...])
    wtab[...] = jnp.concatenate([uhigh, uhigh, ulow, ulow], 0)
    prod_a[...] = dot(lhs[...], wtab[...])

    def one(slot, now, later):
        slot_copy(slot + 1).wait()
        build(slot + 1)

        def part(c, carry):
            at = pl.ds(pl.multiple_of(256 * c, 256), 256)
            later[:, at] = dot(lhs[...], wtab[:, at])
            for b in range(32):
                add_tile(slot, now, c, b)
            return carry

        lax.fori_loop(0, 4, part, 0)

    def two(m, carry):
        one(2 * m, prod_a, prod_b)
        one(2 * m + 1, prod_b, prod_a)
        return carry

    def final(c, carry):
        for b in range(32):
            add_tile(NZ - 1, prod_b, c, b)
        return carry

    lax.fori_loop(0, NZ // 2 - 1, two, 0)
    one(NZ - 2, prod_a, prod_b)
    lax.fori_loop(0, 4, final, 0)

    for q in range(8):
        prod_a[32 * q : 32 * q + 32, :] = acc[:, q, :]
    for k in range(8):
        out[128 * k : 128 * k + 128, :] = prod_a[0:256, 128 * k : 128 * k + 128].T


def image_rows(tiles, where):
    hbm = pl.BlockSpec(memory_space=pl.ANY)
    vmem = pl.BlockSpec(memory_space=pltpu.VMEM)
    return pl.pallas_call(
        rows_kernel,
        out_shape=jax.ShapeDtypeStruct((1024, 256), F32),
        in_specs=[hbm] * 3,
        out_specs=vmem,
        scratch_shapes=[
            pltpu.VMEM((NZ, 4, NX, 8, 512), F32),
            pltpu.VMEM((64, 1024), F32),
            pltpu.VMEM((256, 512), F32),
            pltpu.VMEM((256, 1024), BF),
            pltpu.SMEM((NZ, 128), jnp.int32),
            pltpu.VMEM((1024, 256), BF),
            pltpu.VMEM((1024, 1024), F32),
            pltpu.VMEM((1024, 1024), F32),
            pltpu.VMEM((32, 8, 1024), F32),
            pltpu.SemaphoreType.DMA((2,)),
            pltpu.SemaphoreType.DMA((NZ,)),
        ],
        compiler_params=pltpu.CompilerParams(vmem_limit_bytes=52 << 20),
    )(tiles, where, jnp.asarray(row_table()))


def spread_kernel(rows, out, stage, local, send, recv, there, here, onward, landed):
    bt, ch = lax.axis_index("bt"), lax.axis_index("ch")
    z, x = bt // NX, bt % NX
    y, core = ch // 2, ch % 2
    me = x * NCH + ch

    def at(dx, dy, dc):
        xx, yy, cc = (x + dx) % NX, (y + dy) % 4, (core + dc) % 2
        return xx * NCH + 2 * yy + cc, (z * NX + xx, 2 * yy + cc)

    steps = [(dx, dy, dc) for dx in (2, 1, 3, 0) for dy in (2, 1, 3, 0) for dc in (0, 1)][:-2] + [(0, 0, 1)]
    around = [((2, dy, 1), (3, 0, 0), (1, 0, 0), (3, dy, 1)) for dy in range(4)]
    around += [((dx, 2, 0), (0, 3, 0), (0, 1, 0), (dx, 3, 0)) for dx in range(4)]
    straight = [step for step in steps if step not in [way[0] for way in around]]
    barrier = pltpu.get_barrier_semaphore()
    for step in steps:
        pl.semaphore_signal(barrier, inc=1, device_id=at(*step)[1], device_id_type=MESH)
    own = pltpu.make_async_copy(rows.at[:, me], out.at[me], local)
    own.start()
    pl.semaphore_wait(barrier, len(steps))

    def remote(src, dst, sender, receiver, peer):
        copy = pltpu.make_async_remote_copy(
            src_ref=src,
            dst_ref=dst,
            send_sem=sender,
            recv_sem=receiver,
            device_id=peer,
            device_id_type=MESH,
        )
        copy.start()
        return copy

    first = [
        remote(rows.at[:, at(*goal)[0]], stage.at[j], there.at[j], here.at[j], at(*relay)[1])
        for j, (goal, relay, _, _) in enumerate(around)
    ]
    copies = [
        remote(rows.at[:, at(*goal)[0]], out.at[me], send.at[j], recv.at[j], at(*goal)[1])
        for j, goal in enumerate(straight)
    ]
    for j, (_, _, origin, goal) in enumerate(around):
        first[j].wait_recv()
        copies.append(
            remote(stage.at[j], out.at[at(*origin)[0]], onward.at[j], landed.at[j], at(*goal)[1])
        )
    for copy in copies:
        copy.wait()
    for copy in first:
        copy.wait_send()
    own.wait()


def spread(rows):
    vmem = pl.BlockSpec(memory_space=pltpu.VMEM)
    n = NX * NCH
    dma = pltpu.SemaphoreType.DMA
    return pl.pallas_call(
        spread_kernel,
        out_shape=jax.ShapeDtypeStruct((n, 2, 16, 256), F32),
        in_specs=[vmem],
        out_specs=vmem,
        scratch_shapes=[
            pltpu.VMEM((8, 2, 16, 256), F32),
            dma,
            dma((n - 9,)),
            dma((n - 9,)),
            dma((8,)),
            dma((8,)),
            dma((8,)),
            dma((8,)),
        ],
        compiler_params=pltpu.CompilerParams(
            collective_id=1, has_side_effects=True, vmem_limit_bytes=40 << 20
        ),
    )(rows)


def turn(values):
    n = len(values)
    if n == 1:
        return values
    even, odd = turn(values[0::2]), turn(values[1::2])
    low, high = [], []
    for k in range(n // 2):
        er, ei = even[k]
        xr, xi = odd[k]
        if k == 0:
            tr, ti = xr, xi
        elif 4 * k == n:
            tr, ti = -xi, xr
        else:
            c, s = math.cos(2 * math.pi * k / n), math.sin(2 * math.pi * k / n)
            tr, ti = c * xr - s * xi, c * xi + s * xr
        low.append((er + tr, ei + ti))
        high.append((er - tr, ei - ti))
    return low + high


def columns_kernel(parts, table, twiddle, out, whigh, wlow, vhigh, vlow, mid):
    c, s = table[:, 0:256], table[:, 256:512]
    for rows, both in ((slice(0, 256), table[...]), (slice(256, 512), jnp.concatenate([-s, c], 1))):
        whigh[rows, :], wlow[rows, :] = halves(both)
    lane = lanes((16, 128))

    def one_x(x, carry):
        for r in range(2):
            for h in range(2):
                for j in range(2):
                    pieces = [parts[x * 8 + 4 * h + i, r, :, 128 * j : 128 * j + 128] for i in range(4)]
                    for jj in range(4):
                        got = None
                        for i in range(4):
                            shift = (32 * (i - jj)) % 128
                            piece = pltpu.roll(pieces[i], shift, 1) if shift else pieces[i]
                            got = piece if got is None else jnp.where(lane >= 32 * i, piece, got)
                        high, low = halves(got)
                        rows = pl.ds(pl.multiple_of((x * 8 + 4 * j + jj) * 16, 16), 16)
                        at = slice(256 * r + 128 * h, 256 * r + 128 * h + 128)
                        vhigh[rows, at] = high
                        vlow[rows, at] = low
        return carry

    lax.fori_loop(0, NX, one_x, 0)
    mid[...] = dot(vhigh[...], whigh[...]) + (dot(vlow[...], whigh[...]) + dot(vhigh[...], wlow[...]))
    for a in range(2):
        for e in range(2):
            values = []
            for q in range(SUB):
                rows = slice(16 * q + 8 * a, 16 * q + 8 * a + 8)
                zr = mid[rows, 128 * e : 128 * e + 128]
                zi = mid[rows, 256 + 128 * e : 384 + 128 * e]
                c = twiddle[q : q + 1, 128 * e : 128 * e + 128]
                s = twiddle[q : q + 1, 256 + 128 * e : 384 + 128 * e]
                values.append((c * zr - s * zi, c * zi + s * zr))
            for k, (re, im) in enumerate(turn(values)):
                at = slice(256 * k + 128 * e, 256 * k + 128 * e + 128)
                out[0, 8 * a : 8 * a + 8, at] = re
                out[1, 8 * a : 8 * a + 8, at] = im


def columns(parts):
    vmem = pl.BlockSpec(memory_space=pltpu.VMEM)
    return pl.pallas_call(
        columns_kernel,
        out_shape=jax.ShapeDtypeStruct((2, 16, G), F32),
        in_specs=[vmem] * 3,
        out_specs=vmem,
        scratch_shapes=[
            pltpu.VMEM((512, 512), BF),
            pltpu.VMEM((512, 512), BF),
            pltpu.VMEM((512, 512), BF),
            pltpu.VMEM((512, 512), BF),
            pltpu.VMEM((512, 512), F32),
        ],
        compiler_params=pltpu.CompilerParams(vmem_limit_bytes=40 << 20),
    )(parts, jnp.asarray(column_table()), jnp.asarray(column_twiddle()))


def shards(visibility, cell_offset, station_gain, stations, row_band, tile_offset):
    tiles, where = front(
        visibility,
        cell_offset,
        station_gain.reshape(16, 512),
        stations.T,
        row_band.reshape(128, 128),
        tile_offset.reshape(128, 128),
    )
    rows = image_rows(tiles, where)
    return columns(spread(rows.reshape(2, NX * NCH, 16, 256)))


def solution(mesh):
    return jax.shard_map(
        shards,
        mesh=mesh,
        in_specs=(
            P(None, None, "ch", "bt"),
            P(None, None, "ch", "bt"),
            P(None, "ch", None),
            P("bt", None),
            P(),
            P(),
        ),
        out_specs=P(None, ("bt", "ch"), None),
        check_vma=False,
    )
```

```python
import math

import jax
import jax.numpy as jnp
import numpy as np
from jax import lax
from jax.experimental import pallas as pl
from jax.experimental.pallas import tpu as pltpu
from jax.sharding import PartitionSpec as P

MESH = pl.DeviceIdType.MESH
NZ, NX, NCH = 16, 4, 8
SUB = 32
G = 8192
SPAN = G // NZ
BF = jnp.bfloat16
F32 = jnp.float32


def taper_dft():
    half = SUB // 2
    pos = np.concatenate([np.arange(half, SUB), [0], np.arange(half - 1, 0, -1)])
    x = (pos - half) / SUB
    return np.exp(-2j * np.pi * np.outer(np.arange(SUB), x)) * (np.exp(-4.0 * x * x) / math.sqrt(SUB))[None, :]


def front_table():
    table = taper_dft()
    return np.concatenate([table.real, table.imag], 0).astype(np.float32)


def row_table():
    a = np.arange(G)
    u = np.exp(2j * np.pi * np.outer(a, np.arange(SUB)) / G) @ taper_dft()
    u = u.reshape(NZ, SPAN, SUB).transpose(0, 2, 1)
    w = np.concatenate(
        [np.concatenate([u.real, u.imag], 2), np.concatenate([-u.imag, u.real], 2)], 1
    )
    return w.astype(np.float32)


def column_table():
    ang = 2 * np.pi * (np.outer(np.arange(256), np.arange(256)) % 256) / 256
    return np.concatenate([np.cos(ang), np.sin(ang)], 1).astype(np.float32)


def column_twiddle():
    ang = 2 * np.pi * np.outer(np.arange(SUB), np.arange(256)) / G
    scale = 1.0 / (G * 16.0)
    return (np.concatenate([np.cos(ang), np.sin(ang)], 1) * scale).astype(np.float32)


def trig_coefficients():
    f = 0.5 * np.cos(np.pi * (np.arange(4000) + 0.5) / 4000)
    y = f * f
    cosine = np.polynomial.chebyshev.Chebyshev.fit(y, np.cos(2 * np.pi * f), 7, domain=[0, 0.25])
    sine = np.polynomial.chebyshev.Chebyshev.fit(
        y, np.sin(2 * np.pi * f) / f, 6, domain=[0, 0.25]
    )
    convert = np.polynomial.Polynomial
    return (
        [float(v) for v in cosine.convert(kind=convert).coef],
        [float(v) for v in sine.convert(kind=convert).coef],
    )


COS_C, SIN_C = trig_coefficients()


def horner(coefs, y):
    total = jnp.full_like(y, coefs[-1])
    for value in coefs[-2::-1]:
        total = total * y + value
    return total


def phasor(turns):
    f = turns - jnp.floor(turns + 0.5)
    y = f * f
    return horner(COS_C, y), f * horner(SIN_C, y)


def steps(row, u):
    c, s = phasor(row * u)
    end_c = c[8:9] * c[8:9] - s[8:9] * s[8:9]
    end_s = -2.0 * c[8:9] * s[8:9]
    first = lax.broadcasted_iota(jnp.int32, c.shape, 0) == 0
    return (
        jnp.concatenate([c, jnp.where(first, end_c, c)], 0),
        jnp.concatenate([s, jnp.where(first, end_s, -s)], 0),
    )


def halves(v):
    high = v.astype(BF)
    return high, (v - high.astype(F32)).astype(BF)


def dot(a, b, dims=((1,), (0,))):
    return lax.dot_general(a, b, (dims, ((), ())), preferred_element_type=F32)


def lanes(shape):
    return lax.broadcasted_iota(jnp.int32, shape, 1)


def front_kernel(
    vis_hbm, off_hbm, gain_hbm, st_hbm, band_hbm, place_hbm, ttab_hbm, tiles, where_out,
    vis, off, gain, st, band, place, ttab,
    packed, landed, quant, image, tile,
    load, keep, ch_send, ch_recv, x_send, x_recv, z_send, z_recv,
):
    bt, ch = lax.axis_index("bt"), lax.axis_index("ch")
    z, x = bt // NX, bt % NX
    ch_peer = [(bt, (ch + d) % NCH) for d in range(1, NCH)]
    x_peer = [(z * NX + (x + d) % NX, ch) for d in range(1, NX)]
    right = (((z + 1) % NZ) * NX + x, ch)
    left = (((z + NZ - 1) % NZ) * NX + x, ch)
    barrier = pltpu.get_barrier_semaphore()
    peers = ch_peer + x_peer + [right, left]
    for peer in peers:
        pl.semaphore_signal(barrier, inc=1, device_id=peer, device_id_type=MESH)
    loads = [
        pltpu.make_async_copy(src, dst, load.at[i])
        for i, (src, dst) in enumerate(
            [
                (gain_hbm, gain), (st_hbm, st), (vis_hbm, vis), (off_hbm, off), (band_hbm, band),
                (place_hbm, place), (ttab_hbm, ttab),
            ]
        )
    ]
    for copy in loads:
        copy.start()

    loads[0].wait()
    loads[1].wait()
    g = gain[...]
    g0 = g.astype(BF)
    rest = g - g0.astype(F32)
    g1 = rest.astype(BF)
    g2 = (rest - g1.astype(F32)).astype(BF)
    parts = jnp.concatenate([g0, g1, g2], 0)
    stations = lax.broadcasted_iota(jnp.int32, (512, 256), 0)

    def pick(row):
        hot = jnp.where(stations == st[row : row + 1, :], 1.0, 0.0).astype(BF)
        got = dot(parts, hot)
        got = (got[0:16] + got[16:32]) + got[32:48]
        return got[0:8], got[8:16]

    pr, pi = pick(0)
    qr, qi = pick(1)
    ar = pr * qr + pi * qi
    ai = pi * qr - pr * qi
    loads[2].wait()
    loads[3].wait()
    rows_r, rows_i, rows_u, rows_v = [], [], [], []
    for t in range(4):
        vr, vi = vis[0, t], vis[1, t]
        rows_r.append(vr * ar - vi * ai)
        rows_i.append(vr * ai + vi * ar)
        rows_u.append(off[0, t])
        rows_v.append(off[1, t])
    packed[...] = jnp.concatenate(rows_r + rows_i + rows_u + rows_v, 0).T

    pl.semaphore_wait(barrier, len(peers))
    copies = []
    for d, peer in enumerate(ch_peer):
        copy = pltpu.make_async_remote_copy(
            src_ref=packed.at[pl.ds(pl.multiple_of(peer[1] * 32, 32), 32)],
            dst_ref=landed.at[ch],
            send_sem=ch_send.at[d],
            recv_sem=ch_recv.at[d],
            device_id=peer,
            device_id_type=MESH,
        )
        copy.start()
        copies.append(copy)
    landed[ch] = packed[pl.ds(pl.multiple_of(ch * 32, 32), 32), :]

    for copy in loads[4:7]:
        copy.wait()
    lane16 = lanes((NZ, 128))
    where = None
    for xs in range(NX):
        near, far = pl.ds(2 * xs, NZ, stride=8), pl.ds(2 * xs + 1, NZ, stride=8)
        piece = jnp.where(
            ch // 4 == 0, band[near, :] * 128 + place[near, :], band[far, :] * 128 + place[far, :]
        )
        piece = pltpu.roll(piece, (32 * xs + 128 - 32 * (ch % 4)) % 128, 1)
        where = piece if where is None else jnp.where(lane16 >= 32 * xs, piece, where)
    where_out[...] = where
    for copy in copies:
        copy.wait()

    lane = lanes((32, 128))
    for h in range(2):
        for q in range(4):
            got = None
            for i in range(4):
                shift = (32 * (i - q)) % 128
                piece = landed[4 * h + i]
                if shift:
                    piece = pltpu.roll(piece, shift, 1)
                got = piece if got is None else jnp.where(lane >= 32 * i, piece, got)
            quant[q, :, 128 * h : 128 * h + 128] = got

    xl = lax.broadcasted_iota(jnp.int32, (16, 256), 0).astype(F32) * (1.0 / 32.0)
    sign = jnp.where((lane // 32) % 2 == 0, -1.0, 1.0)

    def one_block(b):
        wr = quant[0, pl.ds(b, 1), :]
        wi = quant[1, pl.ds(b, 1), :]
        u = quant[2, pl.ds(b, 1), :]
        v = quant[3, pl.ds(b, 1), :]
        cu, su = steps(xl, u)
        rr, ri = steps(xl, v)
        lr = wr * cu - wi * su
        li = wr * su + wi * cu
        lrh, lrl = halves(lr)
        lih, lil = halves(li)
        rrh, rrl = halves(rr)
        rih, ril = halves(ri)
        d = dot(
            jnp.concatenate([rrh, rih, rrl, ril], 0),
            jnp.concatenate([lrh, lih, lrl, lil], 0),
            ((1,), (1,)),
        )
        pr_ = d[0:32] + d[64:96]
        pi_ = d[32:64] + d[96:128]
        pr_ = pr_ + pltpu.roll(pr_, 64, 1)
        pi_ = pi_ + pltpu.roll(pi_, 64, 1)
        return pr_ + sign * pltpu.roll(pi_, 32, 1)

    def x_copy(c, d):
        to = (x + d + 1) % NX
        return pltpu.make_async_remote_copy(
            src_ref=tile.at[c, pl.ds(pl.multiple_of(to * 8, 8), 8)],
            dst_ref=tiles.at[z, c, x],
            send_sem=x_send.at[c, d],
            recv_sem=x_recv.at[c, d],
            device_id=x_peer[d],
            device_id_type=MESH,
        )

    sent = {}

    def hop(way, step, c):
        slot = (z + NZ - step) % NZ if way == 0 else (z + step) % NZ
        copy = pltpu.make_async_remote_copy(
            src_ref=tiles.at[slot, c],
            dst_ref=tiles.at[slot, c],
            send_sem=z_send.at[way, step, c],
            recv_sem=z_recv.at[way, step, c],
            device_id=right if way == 0 else left,
            device_id_type=MESH,
        )
        copy.start()
        sent[way, step, c] = copy

    thigh, tlow = halves(ttab[...])
    tparts = jnp.concatenate([thigh, thigh, tlow], 1)
    crossing = {}

    def leave(c):
        for copy in crossing[c]:
            copy.wait()
        for way in range(2):
            hop(way, 0, c)

    for c in range(4):

        def pair(p, carry):
            b = 8 * c + 2 * p
            both = jnp.where(lane < 64, one_block(b), one_block(b + 1))
            image[:, pl.ds(pl.multiple_of(p * 128, 128), 128)] = both
            return carry

        lax.fori_loop(0, 4, pair, 0, unroll=4)
        high, low = halves(image[...])
        ts = dot(tparts, jnp.concatenate([high, low, high], 0))
        for k in range(4):
            at = slice(128 * k, 128 * k + 128)
            tr, ti = ts[0:32, at], ts[32:64, at]
            other = jnp.where(sign < 0, pltpu.roll(ti, 96, 1), pltpu.roll(ti, 32, 1))
            tile[c, :, at] = tr + sign * other
        crossing[c] = [x_copy(c, d) for d in range(NX - 1)]
        for copy in crossing[c]:
            copy.start()
        own = pltpu.make_async_copy(
            tile.at[c, pl.ds(pl.multiple_of(x * 8, 8), 8)], tiles.at[z, c, x], keep.at[c]
        )
        own.start()
        crossing[c].append(own)
        if c:
            leave(c - 1)
    leave(3)

    last = NZ // 2 - 1
    for step in range(1, NZ // 2):
        for c in range(4):
            for way in range(2):
                sent[way, step - 1, c].wait_recv()
                if step < last or (c < 2) == (way == 0):
                    hop(way, step, c)
    for (way, step, c), copy in sent.items():
        if step == last:
            copy.wait_recv()
    for copy in sent.values():
        copy.wait_send()


def front(vis, off, gain, st, band, place):
    hbm = pl.BlockSpec(memory_space=pl.ANY)
    vmem = pl.BlockSpec(memory_space=pltpu.VMEM)
    dma = pltpu.SemaphoreType.DMA
    return pl.pallas_call(
        front_kernel,
        out_shape=[
            jax.ShapeDtypeStruct((NZ, 4, NX, 8, 512), F32),
            jax.ShapeDtypeStruct((NZ, 128), jnp.int32),
        ],
        in_specs=[hbm] * 7,
        out_specs=[hbm, vmem],
        scratch_shapes=[
            pltpu.VMEM((2, 4, 8, 256), F32),
            pltpu.VMEM((2, 4, 8, 256), F32),
            pltpu.VMEM((16, 512), F32),
            pltpu.VMEM((2, 256), jnp.int32),
            pltpu.VMEM((128, 128), jnp.int32),
            pltpu.VMEM((128, 128), jnp.int32),
            pltpu.VMEM((64, 32), F32),
            pltpu.VMEM((256, 128), F32),
            pltpu.VMEM((8, 32, 128), F32),
            pltpu.VMEM((4, 32, 256), F32),
            pltpu.VMEM((32, 512), F32),
            pltpu.VMEM((4, 32, 512), F32),
            dma((7,)),
            dma((4,)),
            dma((NCH - 1,)),
            dma((NCH - 1,)),
            dma((4, NX - 1)),
            dma((4, NX - 1)),
            dma((2, NZ // 2, 4)),
            dma((2, NZ // 2, 4)),
        ],
        compiler_params=pltpu.CompilerParams(
            collective_id=0, has_side_effects=True, vmem_limit_bytes=58 << 20
        ),
    )(vis, off, gain, st, band, place, jnp.asarray(front_table()))


def rows_kernel(
    tiles_hbm, where, utab_hbm, out,
    tiles, utab, phase, wtab, where_s, lhs, prod_a, prod_b, acc, load, fetch,
):
    z = lax.axis_index("bt") // NX
    loads = [
        pltpu.make_async_copy(utab_hbm.at[z], utab, load.at[0]),
        pltpu.make_async_copy(where, where_s, load.at[1]),
    ]

    def slot_copy(slot):
        return pltpu.make_async_copy(tiles_hbm.at[slot], tiles.at[slot], fetch.at[slot])

    slot_copy(0).start()
    for copy in loads:
        copy.start()
    for slot in range(1, NZ):
        slot_copy(slot).start()
    acc[...] = jnp.zeros_like(acc)
    low_half = lanes((8, 128)) < 64

    def build(slot):
        for c in range(4):
            for xs in range(NX):
                for p in range(4):
                    v = tiles[slot, c, xs, :, 128 * p : 128 * p + 128]
                    high = v.astype(BF).astype(F32)
                    rolled = pltpu.roll(v - high, 64, 1)
                    first = jnp.concatenate(
                        [jnp.where(low_half, high, rolled), jnp.where(low_half, high, 0.0)], 1
                    )
                    second = jnp.concatenate(
                        [jnp.where(low_half, rolled, high), jnp.where(low_half, 0.0, high)], 1
                    )
                    k = 256 * c + 64 * xs + 16 * p
                    lhs[k : k + 16, :] = jnp.concatenate([first, second], 0).astype(BF)

    def add_tile(slot, prod, c, b):
        word = where_s[slot, (b // 8) * 32 + c * 8 + b % 8]
        tr, tc = word >> 5, word & 31
        cs, sn = phase[pl.ds(tr, 1), 0:256], phase[pl.ds(tr, 1), 256:512]
        rows = pl.ds(pl.multiple_of(c * 256 + 8 * b, 8), 8)
        for h in range(2):
            re, im = slice(256 * h, 256 * h + 256), slice(512 + 256 * h, 768 + 256 * h)
            pr, pi = prod[rows, re], prod[rows, im]
            acc[tc, :, re] += cs * pr - sn * pi
            acc[tc, :, im] += cs * pi + sn * pr

    for k in range(4):
        tr = lax.broadcasted_iota(jnp.int32, (64, 256), 0) + 64 * k
        turns = (tr * lanes((64, 256)) % 256).astype(F32) * (1.0 / 256.0)
        phase[64 * k : 64 * k + 64, 0:256], phase[64 * k : 64 * k + 64, 256:512] = phasor(turns)
    slot_copy(0).wait()
    build(0)
    for copy in loads:
        copy.wait()
    uhigh, ulow = halves(utab[...])
    wtab[...] = jnp.concatenate([uhigh, uhigh, ulow, ulow], 0)
    prod_a[...] = dot(lhs[...], wtab[...])

    def one(slot, now, later):
        slot_copy(slot + 1).wait()
        build(slot + 1)

        def part(c, carry):
            at = pl.ds(pl.multiple_of(256 * c, 256), 256)
            later[:, at] = dot(lhs[...], wtab[:, at])
            for b in range(32):
                add_tile(slot, now, c, b)
            return carry

        lax.fori_loop(0, 4, part, 0)

    def two(m, carry):
        one(2 * m, prod_a, prod_b)
        one(2 * m + 1, prod_b, prod_a)
        return carry

    def final(c, carry):
        for b in range(32):
            add_tile(NZ - 1, prod_b, c, b)
        return carry

    lax.fori_loop(0, NZ // 2 - 1, two, 0)
    one(NZ - 2, prod_a, prod_b)
    lax.fori_loop(0, 4, final, 0)

    for q in range(8):
        prod_a[32 * q : 32 * q + 32, :] = acc[:, q, :]
    for k in range(8):
        out[128 * k : 128 * k + 128, :] = prod_a[0:256, 128 * k : 128 * k + 128].T


def image_rows(tiles, where):
    hbm = pl.BlockSpec(memory_space=pl.ANY)
    vmem = pl.BlockSpec(memory_space=pltpu.VMEM)
    return pl.pallas_call(
        rows_kernel,
        out_shape=jax.ShapeDtypeStruct((1024, 256), F32),
        in_specs=[hbm] * 3,
        out_specs=vmem,
        scratch_shapes=[
            pltpu.VMEM((NZ, 4, NX, 8, 512), F32),
            pltpu.VMEM((64, 1024), F32),
            pltpu.VMEM((256, 512), F32),
            pltpu.VMEM((256, 1024), BF),
            pltpu.SMEM((NZ, 128), jnp.int32),
            pltpu.VMEM((1024, 256), BF),
            pltpu.VMEM((1024, 1024), F32),
            pltpu.VMEM((1024, 1024), F32),
            pltpu.VMEM((32, 8, 1024), F32),
            pltpu.SemaphoreType.DMA((2,)),
            pltpu.SemaphoreType.DMA((NZ,)),
        ],
        compiler_params=pltpu.CompilerParams(vmem_limit_bytes=52 << 20),
    )(tiles, where, jnp.asarray(row_table()))


def spread_kernel(rows, out, stage, local, send, recv, there, here, onward, landed):
    bt, ch = lax.axis_index("bt"), lax.axis_index("ch")
    z, x = bt // NX, bt % NX
    y, core = ch // 2, ch % 2
    me = x * NCH + ch

    def at(dx, dy, dc):
        xx, yy, cc = (x + dx) % NX, (y + dy) % 4, (core + dc) % 2
        return xx * NCH + 2 * yy + cc, (z * NX + xx, 2 * yy + cc)

    steps = [(dx, dy, dc) for dx in (2, 1, 3, 0) for dy in (2, 1, 3, 0) for dc in (0, 1)][:-2] + [(0, 0, 1)]
    around = [((2, dy, 1), (3, 0, 0), (1, 0, 0), (3, dy, 1)) for dy in range(4)]
    around += [((dx, 2, 0), (0, 3, 0), (0, 1, 0), (dx, 3, 0)) for dx in range(4)]
    straight = [step for step in steps if step not in [way[0] for way in around]]
    barrier = pltpu.get_barrier_semaphore()
    for step in steps:
        pl.semaphore_signal(barrier, inc=1, device_id=at(*step)[1], device_id_type=MESH)
    own = pltpu.make_async_copy(rows.at[:, me], out.at[me], local)
    own.start()
    pl.semaphore_wait(barrier, len(steps))

    def remote(src, dst, sender, receiver, peer):
        copy = pltpu.make_async_remote_copy(
            src_ref=src,
            dst_ref=dst,
            send_sem=sender,
            recv_sem=receiver,
            device_id=peer,
            device_id_type=MESH,
        )
        copy.start()
        return copy

    first = [
        remote(rows.at[:, at(*goal)[0]], stage.at[j], there.at[j], here.at[j], at(*relay)[1])
        for j, (goal, relay, _, _) in enumerate(around)
    ]
    copies = [
        remote(rows.at[:, at(*goal)[0]], out.at[me], send.at[j], recv.at[j], at(*goal)[1])
        for j, goal in enumerate(straight)
    ]
    for j, (_, _, origin, goal) in enumerate(around):
        first[j].wait_recv()
        copies.append(
            remote(stage.at[j], out.at[at(*origin)[0]], onward.at[j], landed.at[j], at(*goal)[1])
        )
    for copy in copies:
        copy.wait()
    for copy in first:
        copy.wait_send()
    own.wait()


def spread(rows):
    vmem = pl.BlockSpec(memory_space=pltpu.VMEM)
    n = NX * NCH
    dma = pltpu.SemaphoreType.DMA
    return pl.pallas_call(
        spread_kernel,
        out_shape=jax.ShapeDtypeStruct((n, 2, 16, 256), F32),
        in_specs=[vmem],
        out_specs=vmem,
        scratch_shapes=[
            pltpu.VMEM((8, 2, 16, 256), F32),
            dma,
            dma((n - 9,)),
            dma((n - 9,)),
            dma((8,)),
            dma((8,)),
            dma((8,)),
            dma((8,)),
        ],
        compiler_params=pltpu.CompilerParams(
            collective_id=1, has_side_effects=True, vmem_limit_bytes=40 << 20
        ),
    )(rows)


def turn(values):
    n = len(values)
    if n == 1:
        return values
    even, odd = turn(values[0::2]), turn(values[1::2])
    low, high = [], []
    for k in range(n // 2):
        er, ei = even[k]
        xr, xi = odd[k]
        if k == 0:
            tr, ti = xr, xi
        elif 4 * k == n:
            tr, ti = -xi, xr
        else:
            c, s = math.cos(2 * math.pi * k / n), math.sin(2 * math.pi * k / n)
            tr, ti = c * xr - s * xi, c * xi + s * xr
        low.append((er + tr, ei + ti))
        high.append((er - tr, ei - ti))
    return low + high


def columns_kernel(parts, table, twiddle, out, whigh, wlow, vhigh, vlow, mid):
    c, s = table[:, 0:256], table[:, 256:512]
    for rows, both in ((slice(0, 256), table[...]), (slice(256, 512), jnp.concatenate([-s, c], 1))):
        whigh[rows, :], wlow[rows, :] = halves(both)
    lane = lanes((16, 128))

    def one_x(x, carry):
        for r in range(2):
            for h in range(2):
                for j in range(2):
                    pieces = [parts[x * 8 + 4 * h + i, r, :, 128 * j : 128 * j + 128] for i in range(4)]
                    for jj in range(4):
                        got = None
                        for i in range(4):
                            shift = (32 * (i - jj)) % 128
                            piece = pltpu.roll(pieces[i], shift, 1) if shift else pieces[i]
                            got = piece if got is None else jnp.where(lane >= 32 * i, piece, got)
                        high, low = halves(got)
                        rows = pl.ds(pl.multiple_of((x * 8 + 4 * j + jj) * 16, 16), 16)
                        at = slice(256 * r + 128 * h, 256 * r + 128 * h + 128)
                        vhigh[rows, at] = high
                        vlow[rows, at] = low
        return carry

    lax.fori_loop(0, NX, one_x, 0)
    mid[...] = dot(vhigh[...], whigh[...]) + (dot(vlow[...], whigh[...]) + dot(vhigh[...], wlow[...]))
    for a in range(2):
        for e in range(2):
            values = []
            for q in range(SUB):
                rows = slice(16 * q + 8 * a, 16 * q + 8 * a + 8)
                zr = mid[rows, 128 * e : 128 * e + 128]
                zi = mid[rows, 256 + 128 * e : 384 + 128 * e]
                c = twiddle[q : q + 1, 128 * e : 128 * e + 128]
                s = twiddle[q : q + 1, 256 + 128 * e : 384 + 128 * e]
                values.append((c * zr - s * zi, c * zi + s * zr))
            for k, (re, im) in enumerate(turn(values)):
                at = slice(256 * k + 128 * e, 256 * k + 128 * e + 128)
                out[0, 8 * a : 8 * a + 8, at] = re
                out[1, 8 * a : 8 * a + 8, at] = im


def columns(parts):
    vmem = pl.BlockSpec(memory_space=pltpu.VMEM)
    return pl.pallas_call(
        columns_kernel,
        out_shape=jax.ShapeDtypeStruct((2, 16, G), F32),
        in_specs=[vmem] * 3,
        out_specs=vmem,
        scratch_shapes=[
            pltpu.VMEM((512, 512), BF),
            pltpu.VMEM((512, 512), BF),
            pltpu.VMEM((512, 512), BF),
            pltpu.VMEM((512, 512), BF),
            pltpu.VMEM((512, 512), F32),
        ],
        compiler_params=pltpu.CompilerParams(vmem_limit_bytes=40 << 20),
    )(parts, jnp.asarray(column_table()), jnp.asarray(column_twiddle()))


def shards(visibility, cell_offset, station_gain, stations, row_band, tile_offset):
    tiles, where = front(
        visibility,
        cell_offset,
        station_gain.reshape(16, 512),
        stations.T,
        row_band.reshape(128, 128),
        tile_offset.reshape(128, 128),
    )
    rows = image_rows(tiles, where)
    return columns(spread(rows.reshape(2, NX * NCH, 16, 256)))


def solution(mesh):
    return jax.shard_map(
        shards,
        mesh=mesh,
        in_specs=(
            P(None, None, "ch", "bt"),
            P(None, None, "ch", "bt"),
            P(None, "ch", None),
            P("bt", None),
            P(),
            P(),
        ),
        out_specs=P(None, ("bt", "ch"), None),
        check_vma=False,
    )
```
